256 devices in a mesh: dp: 8 (over y, z_hi), seq: 32 (over x, z_lo, core).
Axes of the slice: x: 4, y: 4, z: 8 (z_hi: 2, z_lo: 4; z = z_hi * 4 + z_lo), core: 2. Of those that a mesh axis runs over, the one named last changes fastest.
Arguments:
- queries: bfloat16 [32768, 3072], P(('dp', 'seq')), parts along dimension 0, may hold values from -8 to 8
- key_states: bfloat16 [32768, 384], P(('dp', 'seq')), parts along dimension 0, may hold values from -8 to 8
- value_states: bfloat16 [32768, 384], P(('dp', 'seq')), parts along dimension 0, may hold values from -6 to 6
- outputs: bfloat16 [32768, 3072], P(('dp', 'seq')), parts along dimension 0, may hold values from -6 to 6
- out_grad: bfloat16 [32768, 3072], P(('dp', 'seq')), parts along dimension 0, may hold values from -6 to 6
- window_start: int32 [8], P('dp'), parts along dimension 0, may hold values from 0 to 126976
- head_group: int32 [32], replicated, may hold values from 0 to 3, as said below
Outputs:
- query_grad: bfloat16 [32768, 3072], P(('dp', 'seq')), parts along dimension 0
- key_grad: bfloat16 [32768, 384], P(('dp', 'seq')), parts along dimension 0
- value_grad: bfloat16 [32768, 384], P(('dp', 'seq')), parts along dimension 0
The draws below stay inside these ranges and needn't reach their ends.
There are 8 independent parts, one for each index of `dp`. The reference program is written for one: setup_inputs(seed, part) draws one part's arguments, and reference() takes and returns one part's arrays. A program takes and returns all parts, laid end to end along the dimension named above; an argument that names none is the same for every part. Nothing has to cross between parts.
Inputs may be any that keep to these rules, and one draw needn't show every extreme that they name: `head_group`: each of the 4 groups is named by exactly 8 heads.
All inputs are finite; a program needn't handle non-finite values.
Results may differ from the reference program's by a relative error of at most 0.015.
Values may be sent and summed in bfloat16 or wider, within the bound.
A program may use at most 64 MiB of HBM per device.

```python
import jax
import jax.numpy as jnp
from jax import lax

HEADS = 32
GROUPS = 4
HEAD_DIM = 96
ROT_DIM = 24
TOKENS = 4096
SEQ_LEN = 131072


def draw_queries(key, part):
    key = jax.random.fold_in(key, 11)
    field = jnp.clip(jax.random.normal(key, (TOKENS, HEADS, HEAD_DIM), jnp.float32), -4.0, 4.0)
    return field.reshape(TOKENS, HEADS * HEAD_DIM).astype(jnp.bfloat16)


def draw_key_states(key, part):
    key = jax.random.fold_in(key, 23)
    field = jnp.clip(jax.random.normal(key, (TOKENS, GROUPS, HEAD_DIM), jnp.float32), -4.0, 4.0)
    return field.reshape(TOKENS, GROUPS * HEAD_DIM).astype(jnp.bfloat16)


def draw_head_group(key, part):
    key = jax.random.fold_in(key, 37)
    order = jax.random.permutation(key, HEADS).astype(jnp.int32)
    return order // (HEADS // GROUPS)


def shard_levels(rng, dims, shards, least, largest):
    def one(dim, shards_of):
        heights = jax.random.uniform(jax.random.fold_in(jax.random.fold_in(rng, 6), dim), (shards_of,), jnp.float32, least / len(shards), largest / len(shards))
        return jnp.repeat(jnp.exp(heights), dims[dim] // shards_of).reshape((-1,) + (1,) * (len(dims) - dim - 1))

    gain = one(*shards[0])
    for cut in shards[1:]:
        gain = gain * one(*cut)
    return gain


def centred(key, shape, spread, limit, cuts=(), held_as=jnp.bfloat16):
    factor_of = shard_levels(key, shape, cuts, -0.22, 0.18) if cuts else 1.0
    entries = jax.random.normal(key, shape, jnp.float32) * spread * factor_of
    return jnp.minimum(jnp.maximum(entries, -limit), limit).astype(held_as)


def setup_inputs(seed: int = 0, part: int = 0) -> dict:
    streams_of = jax.random.split(jax.random.key(seed), 8)
    own_keys = jax.random.split(jax.random.fold_in(streams_of[7], part), 8)
    return {
        "queries": draw_queries(jax.random.fold_in(jax.random.fold_in(streams_of[7], part), 71), part),
        "key_states": draw_key_states(jax.random.fold_in(jax.random.fold_in(streams_of[7], part), 71), part),
        "value_states": centred(own_keys[2], (TOKENS, GROUPS * HEAD_DIM), 1.0, 6.0, ((0, 32),)),
        "outputs": centred(own_keys[3], (TOKENS, HEADS * HEAD_DIM), 1.0, 6.0, ((0, 32),)),
        "out_grad": centred(own_keys[4], (TOKENS, HEADS * HEAD_DIM), 1.0, 6.0, ((0, 32),)),
        "window_start": jax.random.randint(own_keys[5], (1,), 0, SEQ_LEN - TOKENS + 1).astype(jnp.int32),
        "head_group": draw_head_group(jax.random.fold_in(streams_of[7], 71), part),
    }


def rotate(field, positions, turn_sign):
    half_rot = ROT_DIM // 2
    frequency = 10000.0 ** (-2.0 * jnp.arange(half_rot, dtype=jnp.float32) / ROT_DIM)
    angles = positions[:, None] * frequency[None, :]
    cosine = jnp.cos(angles)[:, None, :]
    sine_part = turn_sign * jnp.sin(angles)[:, None, :]
    first_half = field[..., :half_rot]
    second = field[..., half_rot:ROT_DIM]
    return jnp.concatenate([first_half * cosine - second * sine_part, second * cosine + first_half * sine_part, field[..., ROT_DIM:]], axis=-1)


def reference(queries, key_states, value_states, outputs, out_grad, window_start, head_group):
    score_scale = HEAD_DIM ** -0.5
    token_index = jnp.arange(TOKENS, dtype=jnp.int32)
    positions = (window_start[0] + token_index).astype(jnp.float32)
    query_rot = rotate(queries.reshape(TOKENS, HEADS, HEAD_DIM).astype(jnp.float32), positions, 1.0).astype(jnp.bfloat16)
    key_rot = rotate(key_states.reshape(TOKENS, GROUPS, HEAD_DIM).astype(jnp.float32), positions, 1.0).astype(jnp.bfloat16)
    value_three = value_states.reshape(TOKENS, GROUPS, HEAD_DIM)
    grad_three = out_grad.reshape(TOKENS, HEADS, HEAD_DIM)
    out_three = outputs.reshape(TOKENS, HEADS, HEAD_DIM)
    row_delta = jnp.sum(grad_three.astype(jnp.float32) * out_three.astype(jnp.float32), axis=2)
    causal = token_index[None, :] <= token_index[:, None]

    def one_head(head_id):
        group_id = head_group[head_id]
        query_head = lax.dynamic_index_in_dim(query_rot, head_id, 1, keepdims=False)
        key_head = lax.dynamic_index_in_dim(key_rot, group_id, 1, keepdims=False)
        value_head = lax.dynamic_index_in_dim(value_three, group_id, 1, keepdims=False)
        grad_head = lax.dynamic_index_in_dim(grad_three, head_id, 1, keepdims=False)
        delta_head = lax.dynamic_index_in_dim(row_delta, head_id, 1, keepdims=False)
        scores = jnp.where(causal, jnp.dot(query_head, key_head.T, preferred_element_type=jnp.float32) * score_scale, -jnp.inf)
        row_max = jnp.max(scores, axis=1)
        log_total = row_max + jnp.log(jnp.sum(jnp.exp(scores - row_max[:, None]), axis=1))
        weights = jnp.exp(scores - log_total[:, None])
        weights_half = weights.astype(jnp.bfloat16)
        value_part = jnp.dot(weights_half.T, grad_head, preferred_element_type=jnp.float32)
        dweights = jnp.dot(grad_head, value_head.T, preferred_element_type=jnp.float32)
        dscores = (weights * (dweights - delta_head[:, None])).astype(jnp.bfloat16)
        query_part = jnp.dot(dscores, key_head, preferred_element_type=jnp.float32) * score_scale
        key_part = jnp.dot(dscores.T, query_head, preferred_element_type=jnp.float32) * score_scale
        return query_part, key_part.astype(jnp.bfloat16), value_part.astype(jnp.bfloat16)

    query_all, key_all, value_all = lax.map(one_head, jnp.arange(HEADS, dtype=jnp.int32))
    key_all, value_all = lax.optimization_barrier((key_all, value_all))
    member = (head_group[:, None] == jnp.arange(GROUPS, dtype=jnp.int32)[None, :]).astype(jnp.float32)
    key_sum = jnp.einsum('htd,hg->tgd', key_all.astype(jnp.float32), member, precision=lax.Precision.HIGHEST)
    value_sum = jnp.einsum('htd,hg->tgd', value_all.astype(jnp.float32), member, precision=lax.Precision.HIGHEST)
    query_grad = jnp.transpose(query_all, (1, 0, 2)).astype(jnp.bfloat16).reshape(TOKENS, HEADS * HEAD_DIM)
    key_grad = key_sum.astype(jnp.bfloat16).reshape(TOKENS, GROUPS * HEAD_DIM)
    value_grad = value_sum.astype(jnp.bfloat16).reshape(TOKENS, GROUPS * HEAD_DIM)
    return (query_grad, key_grad, value_grad)
```

```python
import functools
import math

import jax
import jax.numpy as jnp
from jax import lax
from jax.experimental import pallas as pl
from jax.experimental.pallas import tpu as pltpu
from jax.sharding import PartitionSpec as P

HEADS = 32
GROUPS = 4
WIDTH = 96
ROT_DIM = 24
F32 = jnp.float32
BF16 = jnp.bfloat16
LN2 = math.log(2.0)
SCALE = WIDTH**-0.5
NT = (((1,), (1,)), ((), ()))
VM = pltpu.VMEM
SIDE_ROWS = 784


def find_slots(group_ref, slot_ref, count_ref):
    for g in range(GROUPS):
        count_ref[g] = 0
    for h in range(HEADS):
        g = group_ref[h]
        rank = count_ref[g]
        slot_ref[h] = g * 8 + rank
        count_ref[g] = rank + 1


def split3(value):
    high = value.astype(BF16)
    rest = value - high.astype(F32)
    middle = rest.astype(BF16)
    low = (rest - middle.astype(F32)).astype(BF16)
    return high.astype(F32), middle.astype(F32), low.astype(F32)


def prep_kernel(group_ref, q_ref, k_ref, v_ref, o_ref, g_ref, turn_ref, side_ref, kv_ref,
                qt, ot, gt, kt, vt, delta, slot_ref, count_ref):
    find_slots(group_ref, slot_ref, count_ref)

    def flip(j, _):
        lanes = pl.ds(pl.multiple_of(j * 128, 128), 128)
        qt[lanes, :] = q_ref[:, lanes].T
        ot[lanes, :] = o_ref[:, lanes].T
        gt[lanes, :] = g_ref[:, lanes].T
        return 0

    lax.fori_loop(0, 24, flip, 0)
    for j in range(3):
        lanes = slice(j * 128, j * 128 + 128)
        kt[lanes, :] = k_ref[:, lanes].T
        vt[lanes, :] = v_ref[:, lanes].T
    cosine = turn_ref[0]
    sine = turn_ref[1]

    def turned(x):
        head = x[0:ROT_DIM]
        swapped = jnp.concatenate([x[12:24], x[0:12]], axis=0)
        return jnp.concatenate([head * cosine + swapped * sine, x[ROT_DIM:]], axis=0)

    def one_head(h, _):
        rows = pl.ds(pl.multiple_of(h * WIDTH, 32), WIDTH)
        slot = slot_ref[h]
        owner = slot // 4
        place = pl.multiple_of((slot % 4) * WIDTH, 32)
        x = turned(qt[rows, :].astype(F32)) * (SCALE / LN2)
        side_ref[owner, pl.ds(place, WIDTH), :] = x.astype(BF16)
        grad = gt[rows, :]
        side_ref[owner, pl.ds(place + 384, WIDTH), :] = grad
        delta[pl.ds(slot, 1), :] = jnp.sum(
            grad.astype(F32) * ot[rows, :].astype(F32), axis=0, keepdims=True
        )
        return 0

    lax.fori_loop(0, HEADS, one_head, 0)
    for owner in range(8):
        high, middle, low = split3(delta[owner * 4 : owner * 4 + 4, :])
        side_ref[owner, 768:784, :] = jnp.concatenate(
            [high, middle, low, jnp.zeros((4, 128), F32)], axis=0
        ).astype(BF16)
    for g in range(GROUPS):
        rows = slice(g * WIDTH, (g + 1) * WIDTH)
        kv_ref[g, 0:96, :] = turned(kt[rows, :].astype(F32)).astype(BF16)
        kv_ref[g, 96:192, :] = vt[rows, :]


def main_kernel(side_src, kv_src, dq_out, dkv_out,
                side, kv, S, Pm, QT, DO, Kn, Vn, KT, dKa, dVa, DQ,
                dq_src, part, core_in, total_r, total_l, final,
                s_side, r_side, s_kx, r_kx, s_kr, r_kr, s_kl, r_kl, s_kc, r_kc,
                s_dq, r_dq, s_pc, r_pc, s_tr, r_tr, s_tl, r_tl, s_f, r_f):
    me = lax.axis_index("seq")
    x = me // 8
    z = (me // 2) % 4
    c = me % 2
    mine = x * 2 + c

    def at(px, pz, pc):
        return {"seq": px * 8 + pz * 2 + pc}

    def remote(src, dst, send, recv, where):
        return pltpu.make_async_remote_copy(
            src_ref=src, dst_ref=dst, send_sem=send, recv_sem=recv,
            device_id=where, device_id_type=pl.DeviceIdType.MESH,
        )

    peers = [lax.rem(mine + j, 8) for j in range(1, 8)]
    barrier = pltpu.get_barrier_semaphore()
    for p in peers:
        pl.semaphore_signal(barrier, inc=1, device_id=at(p // 2, z, p % 2),
                            device_id_type=pl.DeviceIdType.MESH)

    @pl.when(z > 0)
    def _():
        pl.semaphore_signal(barrier, inc=1, device_id=at(x, z - 1, c),
                            device_id_type=pl.DeviceIdType.MESH)

    @pl.when(z < 3)
    def _():
        pl.semaphore_signal(barrier, inc=1, device_id=at(x, z + 1, c),
                            device_id_type=pl.DeviceIdType.MESH)

    pl.semaphore_wait(barrier, 7 + jnp.minimum(z, 1) + jnp.minimum(3 - z, 1))

    kx = []
    for j in range(1, 4):
        px = lax.rem(x + j, 4)
        copy = remote(kv_src.at[px], kv.at[z, c, x], s_kx.at[j], r_kx.at[x], at(px, z, c))
        copy.start()
        kx.append(copy)
    kv[z, c, x] = kv_src[x]
    moved = []
    for p in peers:
        copy = remote(side_src.at[p], side.at[mine], s_side.at[p], r_side.at[mine], at(p // 2, z, p % 2))
        copy.start()
        moved.append(copy)
    side[mine] = side_src[mine]
    for j in range(1, 4):
        px = lax.rem(x + j, 4)
        remote(kv_src.at[px], kv.at[z, c, px], s_kx.at[j], r_kx.at[px], at(px, z, c)).wait_recv()

    def to_core(b):
        return remote(kv.at[b, c], kv.at[b, c], s_kc.at[b], r_kc.at[b], at(x, z, 1 - c))

    def to_right(b):
        return remote(kv.at[b, c], kv.at[b, c], s_kr.at[b], r_kr.at[b], at(x, z + 1, c))

    def to_left(b):
        return remote(kv.at[b, c], kv.at[b, c], s_kl.at[b], r_kl.at[b], at(x, z - 1, c))

    @pl.when(z < 3)
    def _():
        to_right(z).start()

    @pl.when(z > 0)
    def _():
        to_left(z).start()

    to_core(z).start()
    for step in range(1, 4):
        low = z - step

        @pl.when(low >= 0)
        def _():
            to_right(low).wait_recv()

            @pl.when(z < 3)
            def _():
                to_right(low).start()

            to_core(low).start()

        high = z + step

        @pl.when(high <= 3)
        def _():
            to_left(high).wait_recv()

            @pl.when(z > 0)
            def _():
                to_left(high).start()

            to_core(high).start()

    for b in range(4):
        remote(kv.at[b, c], kv.at[b, 1 - c], s_kc.at[b], r_kc.at[b], at(x, z, 1 - c)).wait_recv()
        to_core(b).wait_send()

        @pl.when((b <= z) & (z < 3))
        def _():
            to_right(b).wait_send()

        @pl.when((b >= z) & (z > 0))
        def _():
            to_left(b).wait_send()

    for copy in kx:
        copy.wait_send()
    for p, copy in zip(peers, moved):
        remote(side_src.at[p], side.at[p], s_side.at[p], r_side.at[p], at(p // 2, z, p % 2)).wait_recv()
        copy.wait_send()

    one_rows = (lax.broadcasted_iota(jnp.int32, (32, 128), 0) < 3).astype(BF16)
    zero_rows = jnp.zeros((32, 128), BF16)
    for half in range(2):
        lanes = slice(half * 128, half * 128 + 128)

        def stage(i, _):
            b = i // 4
            px = i % 4
            block = kv[b, half, px]
            keys = block[0:96]
            KT[px * 4 + b, :, lanes] = keys
            Kn[px * 4 + b, lanes, :] = jnp.concatenate([keys, zero_rows], 0).T
            Vn[px * 4 + b, lanes, :] = jnp.concatenate([block[96:192], one_rows], 0).T
            return 0

        lax.fori_loop(0, 16, stage, 0)

    def clear(i, _):
        dKa[i] = jnp.zeros((96, 256), F32)
        dVa[i] = jnp.zeros((96, 256), F32)
        return 0

    lax.fori_loop(0, 16, clear, 0)
    allowed = lax.broadcasted_iota(jnp.int32, (256, 256), 0) <= lax.broadcasted_iota(
        jnp.int32, (256, 256), 1
    )
    row_id = lax.broadcasted_iota(jnp.int32, (32, 128), 0)
    QT[96:128, :] = jnp.zeros((32, 1024), BF16)

    def query_block(qx, _):
        for h in range(4):
            for half in range(2):
                start = h * 256 + half * 128
                QT[0:96, start : start + 128] = side[qx * 2 + half, h * 96 : h * 96 + 96, :]
        count = qx * 4 + z + 1

        def scores(kb, state):
            result = []
            for h in range(4):
                lanes = slice(h * 256, h * 256 + 256)
                s = jnp.dot(Kn[kb], QT[:, lanes], preferred_element_type=F32)
                S[kb, :, lanes] = s
                result.append(jnp.maximum(state[h], jnp.max(s.reshape(32, 8, 256), axis=0)))
            return tuple(result)

        state = tuple(jnp.full((8, 256), -1e30, F32) for _ in range(4))
        state = lax.fori_loop(0, count - 1, scores, state)
        top = []
        for h in range(4):
            lanes = slice(h * 256, h * 256 + 256)
            s = jnp.dot(Kn[count - 1], QT[:, lanes], preferred_element_type=F32)
            s = jnp.where(allowed, s, -1e30)
            S[count - 1, :, lanes] = s
            high = jnp.maximum(state[h], jnp.max(s.reshape(32, 8, 256), axis=0))
            top.append(jnp.max(high, axis=0, keepdims=True))

        def weigh(kb, sums):
            result = []
            for h in range(4):
                lanes = slice(h * 256, h * 256 + 256)
                p = jnp.exp2(S[kb, :, lanes] - top[h])
                Pm[kb, :, lanes] = p.astype(BF16)
                result.append(sums[h] + jnp.sum(p.reshape(32, 8, 256), axis=0))
            return tuple(result)

        sums = lax.fori_loop(0, count, weigh, tuple(jnp.zeros((8, 256), F32) for _ in range(4)))
        for h in range(4):
            share = 1.0 / jnp.sum(sums[h], axis=0, keepdims=True)
            for half in range(2):
                part_share = share[:, half * 128 : half * 128 + 128]
                start = h * 256 + half * 128
                grad = side[qx * 2 + half, 384 + h * 96 : 480 + h * 96, :]
                DO[0:96, start : start + 128] = (grad.astype(F32) * part_share).astype(BF16)
                d = side[qx * 2 + half, 768:784, :].astype(F32)
                d = -(d[h : h + 1] + d[4 + h : 5 + h] + d[8 + h : 9 + h]) * part_share
                high, middle, low = split3(d)
                DO[96:128, start : start + 128] = jnp.where(
                    row_id == 0, high, jnp.where(row_id == 1, middle, jnp.where(row_id == 2, low, 0.0))
                ).astype(BF16)
        DQ[...] = jnp.zeros((96, 1024), F32)

        def gradient(kb, _):
            pieces = []
            for h in range(4):
                lanes = slice(h * 256, h * 256 + 256)
                dp = jnp.dot(Vn[kb], DO[:, lanes], preferred_element_type=F32)
                pieces.append((Pm[kb, :, lanes].astype(F32) * dp).astype(BF16))
            ds = jnp.concatenate(pieces, axis=1)
            dVa[kb] += lax.dot_general(DO[0:96, :], Pm[kb], NT, preferred_element_type=F32)
            dKa[kb] += lax.dot_general(QT[0:96, :], ds, NT, preferred_element_type=F32)
            DQ[...] += jnp.dot(KT[kb], ds, preferred_element_type=F32)
            return 0

        lax.fori_loop(0, count, gradient, 0)
        for h in range(4):
            for half in range(2):
                start = h * 256 + half * 128
                dq_src[qx * 2 + half, h * 96 : h * 96 + 96, :] = (
                    DQ[:, start : start + 128] * SCALE
                ).astype(BF16)
        return 0

    lax.fori_loop(0, 4, query_block, 0)
    for half in range(2):
        lanes = slice(half * 128, half * 128 + 128)

        def finish(i, _):
            b = i // 4
            px = i % 4
            part[b, half, px, 0:96, :] = (dKa[px * 4 + b, :, lanes] * LN2).astype(BF16)
            part[b, half, px, 96:192, :] = dVa[px * 4 + b, :, lanes].astype(BF16)
            return 0

        lax.fori_loop(0, 16, finish, 0)

    moved = []
    for p in peers:
        copy = remote(dq_src.at[p], dq_out.at[mine], s_dq.at[p], r_dq.at[mine], at(p // 2, z, p % 2))
        copy.start()
        moved.append(copy)
    order = (3, 0, 2, 1)
    swaps = {}
    for b in order:
        swaps[b] = remote(part.at[b, 1 - c], core_in.at[b], s_pc.at[b], r_pc.at[b], at(x, z, 1 - c))
        swaps[b].start()
    dq_out[mine] = dq_src[mine]
    for b in order:
        swaps[b].wait()

        def add(i, _):
            part[b, c, i] = (part[b, c, i].astype(F32) + core_in[b, i].astype(F32)).astype(BF16)
            return 0

        lax.fori_loop(0, 4, add, 0)

    def pass_right(t):
        return remote(total_r.at[t], total_r.at[t], s_tr.at[t], r_tr.at[t], at(x, z + 1, c))

    def pass_left(t):
        return remote(total_l.at[t], total_l.at[t], s_tl.at[t], r_tl.at[t], at(x, z - 1, c))

    def hop(total, t, first, descriptor):
        @pl.when(first)
        def _():
            total[t] = part[t, c]

        @pl.when(jnp.logical_not(first))
        def _():
            descriptor(t).wait_recv()

            def add(i, _):
                total[t, i] = (total[t, i].astype(F32) + part[t, c, i].astype(F32)).astype(BF16)
                return 0

            lax.fori_loop(0, 4, add, 0)

        descriptor(t).start()

    for right, left in ((3, 0), (2, 1), (1, 2)):
        @pl.when(z < right)
        def _():
            hop(total_r, right, z == 0, pass_right)

        @pl.when(z > left)
        def _():
            hop(total_l, left, z == 3, pass_left)

    def gather(i, _):
        final[i] = part[z, c, i].astype(F32)
        return 0

    lax.fori_loop(0, 4, gather, 0)

    @pl.when(z > 0)
    def _():
        pass_right(z).wait_recv()

        def add(i, _):
            final[i] += total_r[z, i].astype(F32)
            return 0

        lax.fori_loop(0, 4, add, 0)

    @pl.when(z < 3)
    def _():
        pass_left(z).wait_recv()

        def add(i, _):
            final[i] += total_l[z, i].astype(F32)
            return 0

        lax.fori_loop(0, 4, add, 0)

    def settle(i, _):
        core_in[0, i] = final[i].astype(BF16)
        return 0

    lax.fori_loop(0, 4, settle, 0)
    sent = []
    for j in range(1, 4):
        px = lax.rem(x + j, 4)
        copy = remote(core_in.at[0, px], dkv_out.at[x], s_f.at[j], r_f.at[x], at(px, z, c))
        copy.start()
        sent.append(copy)
    dkv_out[x] = core_in[0, x]
    for t in range(4):
        @pl.when(z < t)
        def _():
            pass_right(t).wait_send()

        @pl.when(z > t)
        def _():
            pass_left(t).wait_send()

    for p, copy in zip(peers, moved):
        remote(dq_src.at[p], dq_out.at[p], s_dq.at[p], r_dq.at[p], at(p // 2, z, p % 2)).wait_recv()
        copy.wait_send()
    for j, copy in zip(range(1, 4), sent):
        px = lax.rem(x + j, 4)
        remote(core_in.at[0, px], dkv_out.at[px], s_f.at[j], r_f.at[px], at(px, z, c)).wait_recv()
        copy.wait_send()


def finish_kernel(group_ref, dq_ref, dkv_ref, q_ref, k_ref, v_ref, qt, kt, vt, slot_ref, count_ref):
    find_slots(group_ref, slot_ref, count_ref)

    def one_head(h, _):
        slot = slot_ref[h]
        place = pl.multiple_of((slot % 4) * WIDTH, 32)
        qt[pl.ds(pl.multiple_of(h * WIDTH, 32), WIDTH), :] = dq_ref[slot // 4, pl.ds(place, WIDTH), :]
        return 0

    lax.fori_loop(0, HEADS, one_head, 0)
    for g in range(GROUPS):
        kt[g * WIDTH : (g + 1) * WIDTH, :] = dkv_ref[g, 0:96, :]
        vt[g * WIDTH : (g + 1) * WIDTH, :] = dkv_ref[g, 96:192, :]

    def flip(j, _):
        lanes = pl.ds(pl.multiple_of(j * 128, 128), 128)
        q_ref[:, lanes] = qt[lanes, :].T
        return 0

    lax.fori_loop(0, 24, flip, 0)
    for j in range(3):
        lanes = slice(j * 128, j * 128 + 128)
        k_ref[:, lanes] = kt[lanes, :].T
        v_ref[:, lanes] = vt[lanes, :].T


def per_device(queries, key_states, value_states, outputs, out_grad, window_start, head_group):
    in_vmem = pl.BlockSpec(memory_space=VM)
    in_smem = pl.BlockSpec(memory_space=pltpu.SMEM)
    shape = jax.ShapeDtypeStruct
    me = lax.axis_index("seq")
    position = (window_start[0] + me * 128 + jnp.arange(128, dtype=jnp.int32)).astype(F32)
    half = ROT_DIM // 2
    frequency = 10000.0 ** (-2.0 * jnp.arange(half, dtype=F32) / ROT_DIM)
    angles = position[None, :] * frequency[:, None]
    cosine, sine = jnp.cos(angles), jnp.sin(angles)
    turn = jnp.stack([jnp.concatenate([cosine, cosine], 0), jnp.concatenate([-sine, sine], 0)])
    smem = pltpu.SMEM
    side, kv = pl.pallas_call(
        prep_kernel,
        out_shape=(shape((8, SIDE_ROWS, 128), BF16), shape((4, 192, 128), BF16)),
        in_specs=[in_smem] + [in_vmem] * 6,
        out_specs=(in_vmem, in_vmem),
        scratch_shapes=[VM((3072, 128), BF16)] * 3 + [VM((384, 128), BF16)] * 2
        + [VM((32, 128), F32), smem((32,), jnp.int32), smem((4,), jnp.int32)],
        compiler_params=pltpu.CompilerParams(vmem_limit_bytes=24 << 20),
    )(head_group, queries, key_states, value_states, outputs, out_grad, turn)
    dma = pltpu.SemaphoreType.DMA
    dq, dkv = pl.pallas_call(
        main_kernel,
        out_shape=(shape((8, 384, 128), BF16), shape((4, 192, 128), BF16)),
        in_specs=[in_vmem] * 2,
        out_specs=(in_vmem, in_vmem),
        scratch_shapes=[
            VM((8, SIDE_ROWS, 128), BF16), VM((4, 2, 4, 192, 128), BF16),
            VM((16, 256, 1024), F32), VM((16, 256, 1024), BF16),
            VM((128, 1024), BF16), VM((128, 1024), BF16),
            VM((16, 256, 128), BF16), VM((16, 256, 128), BF16), VM((16, 96, 256), BF16),
            VM((16, 96, 256), F32), VM((16, 96, 256), F32), VM((96, 1024), F32),
            VM((8, 384, 128), BF16), VM((4, 2, 4, 192, 128), BF16), VM((4, 4, 192, 128), BF16),
            VM((4, 4, 192, 128), BF16), VM((4, 4, 192, 128), BF16), VM((4, 192, 128), F32),
        ] + [dma((8,))] * 2 + [dma((4,))] * 8 + [dma((8,))] * 2 + [dma((4,))] * 8,
        compiler_params=pltpu.CompilerParams(
            collective_id=0, has_side_effects=True, vmem_limit_bytes=60 << 20
        ),
    )(side, kv)
    return pl.pallas_call(
        finish_kernel,
        out_shape=(shape((128, 3072), BF16), shape((128, 384), BF16), shape((128, 384), BF16)),
        in_specs=[in_smem, in_vmem, in_vmem],
        out_specs=(in_vmem, in_vmem, in_vmem),
        scratch_shapes=[VM((3072, 128), BF16)] + [VM((384, 128), BF16)] * 2
        + [smem((32,), jnp.int32), smem((4,), jnp.int32)],
        compiler_params=pltpu.CompilerParams(vmem_limit_bytes=24 << 20),
    )(head_group, dq, dkv)


def solution(mesh):
    rows = P(("dp", "seq"), None)
    return jax.shard_map(
        per_device,
        mesh=mesh,
        in_specs=(rows, rows, rows, rows, rows, P("dp"), P()),
        out_specs=(rows, rows, rows),
        check_vma=False,
    )
```

```python
import math

import jax
import jax.numpy as jnp
from jax import lax
from jax.experimental import pallas as pl
from jax.experimental.pallas import tpu as pltpu
from jax.sharding import PartitionSpec as P

HEADS = 32
GROUPS = 4
WIDTH = 96
ROT_DIM = 24
F32 = jnp.float32
BF16 = jnp.bfloat16
LN2 = math.log(2.0)
SCALE = WIDTH**-0.5
NT = (((1,), (1,)), ((), ()))
VM = pltpu.VMEM
GRAD_ROWS = 400


def split3(value):
    high = value.astype(BF16)
    rest = value - high.astype(F32)
    middle = rest.astype(BF16)
    low = (rest - middle.astype(F32)).astype(BF16)
    return high.astype(F32), middle.astype(F32), low.astype(F32)


def kernel(perm, slot_of, turn, q_hbm, k_hbm, v_hbm, o_hbm, g_hbm, dq_hbm, dk_hbm, dv_hbm,
           q_in, g_in, o_in, k_in, v_in, qt, gt, ot, kt, vt, dq_buf, dk_buf, dv_buf,
           ksrc, vsrc, kin, vin, qsrc, gsrc, qin, gin,
           S, bias, Pm, D, QT, DO, Kn, Vn, KT, dKa, dVa, DQ, mrun, mfin, share,
           dq_src, dq_in, part, cin, zin, tot, fin,
           s_in, s_out, s_q, r_q, s_g, r_g, s_kx, r_kx, s_vx, r_vx, s_kz, r_kz, s_kc, r_kc,
           s_vz, r_vz, s_vc, r_vc, s_d, r_d, s_p, r_p, s_z, r_z, s_f, r_f):
    me = lax.axis_index("seq")
    x = me // 8
    z = (me // 2) % 4
    c = me % 2
    mine = x * 2 + c
    mesh_id = pl.DeviceIdType.MESH
    mult = pl.multiple_of

    def at(px, pz, pc):
        return {"seq": px * 8 + pz * 2 + pc}

    def owner_at(p):
        return at(p // 2, z, p % 2)

    def remote(src, dst, send, recv, where):
        return pltpu.make_async_remote_copy(
            src_ref=src, dst_ref=dst, send_sem=send, recv_sem=recv,
            device_id=where, device_id_type=mesh_id,
        )

    def loads():
        pairs = ((k_hbm, k_in), (v_hbm, v_in), (q_hbm, q_in), (g_hbm, g_in), (o_hbm, o_in))
        return [pltpu.make_async_copy(a, b, s_in.at[i]) for i, (a, b) in enumerate(pairs)]

    incoming = loads()
    for copy in incoming:
        copy.start()
    barrier = pltpu.get_barrier_semaphore()
    for j in range(1, 8):
        pl.semaphore_signal(barrier, inc=1, device_id=owner_at(lax.rem(mine + j, 8)), device_id_type=mesh_id)
    for j in range(1, 4):
        pl.semaphore_signal(barrier, inc=1, device_id=at(x, lax.rem(z + j, 4), c), device_id_type=mesh_id)

    cosine = turn[0]
    sine = turn[1]

    def turned(rows):
        first = rows[0:ROT_DIM]
        swapped = jnp.concatenate([first[12:24], first[0:12]], axis=0)
        return jnp.concatenate([first * cosine + swapped * sine, rows[ROT_DIM:]], axis=0)

    def k_along_x(px, land):
        return remote(ksrc.at[px], kin.at[z, c, land], s_kx.at[px], r_kx.at[land], at(px, z, c))

    def v_along_x(px, land):
        return remote(vsrc.at[px], vin.at[z, c, land], s_vx.at[px], r_vx.at[land], at(px, z, c))

    def k_along_z(px, pz, land):
        return remote(kin.at[land, c, px], kin.at[land, c, px], s_kz.at[px * 4 + pz],
                      r_kz.at[px * 4 + land], at(x, pz, c))

    def k_to_core(px, land):
        return remote(kin.at[:, land, px], kin.at[:, land, px], s_kc.at[px], r_kc.at[px], at(x, z, 1 - c))

    def v_along_z(pz, land):
        return remote(vin.at[land, c], vin.at[land, c], s_vz.at[pz], r_vz.at[land], at(x, pz, c))

    def v_to_core(land):
        return remote(vin.at[:, land], vin.at[:, land], s_vc.at[0], r_vc.at[0], at(x, z, 1 - c))

    def q_move(p, land):
        return remote(qsrc.at[p], qin.at[land], s_q.at[p], r_q.at[land], owner_at(p))

    def g_move(p, land):
        return remote(gsrc.at[p], gin.at[land], s_g.at[p], r_g.at[land], owner_at(p))

    def dq_move(p, land):
        return remote(dq_src.at[p], dq_in.at[pl.ds(land * 4, 4)], s_d.at[p], r_d.at[land], owner_at(p))

    def part_move(px):
        return remote(part.at[px, 1 - c], cin.at[px], s_p.at[px], r_p.at[px], at(x, z, 1 - c))

    def sum_along_z(px, pz, land):
        return remote(part.at[px, c, pz], zin.at[px, land], s_z.at[px * 4 + pz], r_z.at[px * 4 + land], at(x, pz, c))

    def total_move(px, land):
        return remote(tot.at[px], fin.at[land], s_f.at[px], r_f.at[land], at(px, z, c))

    def over_x(action):
        for j in range(1, 4):
            action(lax.rem(x + j, 4))

    def over_z(action):
        for j in range(1, 4):
            action(lax.rem(z + j, 4))

    incoming[0].wait()
    for j in range(3):
        lanes = slice(j * 128, j * 128 + 128)
        kt[lanes, :] = k_in[:, lanes].T
    for g in range(GROUPS):
        ksrc[g] = turned(kt[g * WIDTH : (g + 1) * WIDTH, :].astype(F32)).astype(BF16)
    pl.semaphore_wait(barrier, 10)
    over_x(lambda px: k_along_x(px, x).start())
    kin[z, c, x] = ksrc[x]
    incoming[1].wait()
    for j in range(3):
        lanes = slice(j * 128, j * 128 + 128)
        vt[lanes, :] = v_in[:, lanes].T
    for g in range(GROUPS):
        vsrc[g] = vt[g * WIDTH : (g + 1) * WIDTH, :]

    incoming[2].wait()

    def flip_q(j, _):
        rows = q_in[:, pl.ds(mult(j * 384, 128), 384)].T
        for i in range(4):
            qt[j * 4 + i] = rows[i * WIDTH : (i + 1) * WIDTH]
        return 0

    lax.fori_loop(0, 8, flip_q, 0)

    def send_q(j, _):
        p = lax.rem(mine + j, 8)
        for i in range(4):
            rows = qt[perm[p * 4 + i]]
            qsrc[p, i * WIDTH : (i + 1) * WIDTH, :] = (turned(rows.astype(F32)) * (SCALE / LN2)).astype(BF16)

        @pl.when(j < 8)
        def _():
            q_move(p, mine).start()

        return 0

    lax.fori_loop(1, 9, send_q, 0)
    qin[mine] = qsrc[mine]

    over_x(lambda px: k_along_x(px, px).wait_recv())

    def spread_k(px, _):
        over_z(lambda pz: k_along_z(px, pz, z).start())
        return 0

    lax.fori_loop(0, 4, spread_k, 0)
    over_x(lambda px: v_along_x(px, x).start())
    vin[z, c, x] = vsrc[x]

    incoming[3].wait()
    incoming[4].wait()

    def flip_g(j, _):
        lanes = pl.ds(mult(j * 384, 128), 384)
        grads = g_in[:, lanes].T
        outs = o_in[:, lanes].T
        for i in range(4):
            gt[j * 4 + i] = grads[i * WIDTH : (i + 1) * WIDTH]
            ot[j * 4 + i] = outs[i * WIDTH : (i + 1) * WIDTH]
        return 0

    lax.fori_loop(0, 8, flip_g, 0)

    def send_g(j, _):
        p = lax.rem(mine + j, 8)
        deltas = []
        for i in range(4):
            head = perm[p * 4 + i]
            grad = gt[head]
            gsrc[p, i * WIDTH : (i + 1) * WIDTH, :] = grad
            deltas.append(jnp.sum(grad.astype(F32) * ot[head].astype(F32), axis=0, keepdims=True))
        high, middle, low = split3(jnp.concatenate(deltas, axis=0))
        gsrc[p, 384:400, :] = jnp.concatenate(
            [high, middle, low, jnp.zeros((4, 128), F32)], axis=0
        ).astype(BF16)

        @pl.when(j < 8)
        def _():
            g_move(p, mine).start()

        return 0

    lax.fori_loop(1, 9, send_g, 0)
    gin[mine] = gsrc[mine]

    def make_bias(i, _):
        rows = pl.ds(mult(i * 256, 256), 256)
        key_id = lax.broadcasted_iota(jnp.int32, (256, 256), 0) + (i - z) * 256
        bias[rows, :] = jnp.where(key_id <= lax.broadcasted_iota(jnp.int32, (256, 256), 1), 0.0, -1e30)
        return 0

    lax.fori_loop(0, 4, make_bias, 0)

    def clear(i, _):
        dKa[i] = jnp.zeros((96, 1024), F32)
        dVa[i] = jnp.zeros((96, 1024), F32)
        return 0

    lax.fori_loop(0, 4, clear, 0)
    QT[96:128, :] = jnp.zeros((32, 1024), BF16)

    def share_k(px, _):
        over_z(lambda pz: k_along_z(px, pz, pz).wait_recv())
        k_to_core(px, c).start()
        return 0

    lax.fori_loop(0, 4, share_k, 0)
    over_x(lambda px: v_along_x(px, px).wait_recv())
    over_z(lambda pz: v_along_z(pz, z).start())

    heads = [slice(h * 256, h * 256 + 256) for h in range(4)]
    one_rows = (lax.broadcasted_iota(jnp.int32, (32, 128), 0) < 3).astype(BF16)
    zero_rows = jnp.zeros((32, 128), BF16)

    def load_queries(qx):
        for h in range(4):
            for half in range(2):
                start = h * 256 + half * 128
                QT[0:96, start : start + 128] = qin[qx * 2 + half, h * 96 : h * 96 + 96, :]

    def weights_of(qx, _):
        k_to_core(qx, 1 - c).wait_recv()
        for half in range(2):
            p = qx * 2 + half

            @pl.when(p != mine)
            def _():
                q_move(p, p).wait_recv()

        for b in range(8):
            lanes = slice(b * 128, b * 128 + 128)
            keys = kin[b // 2, b % 2, qx]
            KT[qx, :, lanes] = keys
            Kn[qx, lanes, :] = jnp.concatenate([keys, zero_rows], 0).T
        load_queries(qx)
        first = qx * (qx + 1) // 2

        def block(px, state, diagonal):
            top, total = state[:4], state[4:]
            new_top, new_total = [], []
            for h in range(4):
                s = jnp.dot(Kn[px], QT[:, heads[h]], preferred_element_type=F32)
                if diagonal:
                    s = s + bias[...]
                S[:, heads[h]] = s
                high = jnp.max(jnp.max(s.reshape(128, 8, 256), axis=0), axis=0, keepdims=True)
                new_top.append(jnp.maximum(top[h], high))
            for h in range(4):
                p = jnp.exp2(S[:, heads[h]] - new_top[h])
                Pm[first + px, :, heads[h]] = p.astype(BF16)
                new_total.append(
                    total[h] * jnp.exp2(top[h] - new_top[h]) + jnp.sum(p.reshape(128, 8, 256), axis=0)
                )
                mrun[first + px, :, heads[h]] = new_top[h]
            return tuple(new_top) + tuple(new_total)

        state = tuple(jnp.full((1, 256), -1e30, F32) for _ in range(4)) + tuple(
            jnp.zeros((8, 256), F32) for _ in range(4)
        )
        state = lax.fori_loop(0, qx, lambda px, st: block(px, st, False), state)
        state = block(qx, state, True)
        for h in range(4):
            mfin[qx, :, heads[h]] = state[h]
            share[qx, :, heads[h]] = 1.0 / jnp.sum(state[4 + h], axis=0, keepdims=True)

        @pl.when(qx == 2)
        def _():
            over_z(lambda pz: v_along_z(pz, pz).wait_recv())
            v_to_core(c).start()

        return 0

    lax.fori_loop(0, 4, weights_of, 0)
    v_to_core(1 - c).wait_recv()

    def stage_v(px, _):
        for b in range(8):
            lanes = slice(b * 128, b * 128 + 128)
            Vn[px, lanes, :] = jnp.concatenate([vin[b // 2, b % 2, px], one_rows], 0).T
        return 0

    lax.fori_loop(0, 4, stage_v, 0)
    row_id = lax.broadcasted_iota(jnp.int32, (32, 128), 0)

    def reduce_cores(px):
        part_move(px).wait()

        def add(b, _):
            part[px, c, b] = (part[px, c, b].astype(F32) + cin[px, b].astype(F32)).astype(BF16)
            return 0

        lax.fori_loop(0, 4, add, 0)
        over_z(lambda pz: sum_along_z(px, pz, z).start())

    def reduce_z(px):
        over_z(lambda pz: sum_along_z(px, pz, pz).wait_recv())
        value = part[px, c, z].astype(F32)
        for j in range(1, 4):
            value = value + zin[px, lax.rem(z + j, 4)].astype(F32)
        tot[px] = value.astype(BF16)

        @pl.when(px != x)
        def _():
            total_move(px, x).start()

        @pl.when(px == x)
        def _():
            fin[x] = tot[px]

    def gradients_of(i, _):
        qx = 3 - i
        for half in range(2):
            p = qx * 2 + half

            @pl.when(p != mine)
            def _():
                g_move(p, p).wait_recv()

        load_queries(qx)
        DQ[...] = jnp.zeros((96, 1024), F32)
        first = qx * (qx + 1) // 2

        def block(px, _):
            factor = jnp.exp2(mrun[first + px] - mfin[qx]) * share[qx]
            for h in range(4):
                for half in range(2):
                    start = h * 256 + half * 128
                    scale = factor[:, start : start + 128]
                    grad = gin[qx * 2 + half, h * 96 : h * 96 + 96, :]
                    DO[0:96, start : start + 128] = (grad.astype(F32) * scale).astype(BF16)
                    d = gin[qx * 2 + half, 384:400, :].astype(F32)
                    d = -(d[h : h + 1] + d[4 + h : 5 + h] + d[8 + h : 9 + h]) * scale
                    high, middle, low = split3(d)
                    DO[96:128, start : start + 128] = jnp.where(
                        row_id == 0, high, jnp.where(row_id == 1, middle, jnp.where(row_id == 2, low, 0.0))
                    ).astype(BF16)
            for h in range(4):
                for r in range(4):
                    rows = slice(r * 256, r * 256 + 256)
                    dp = jnp.dot(Vn[px, rows, :], DO[:, heads[h]], preferred_element_type=F32)
                    D[rows, heads[h]] = (Pm[first + px, rows, heads[h]].astype(F32) * dp).astype(BF16)
                dVa[px] += lax.dot_general(DO[0:96, heads[h]], Pm[first + px, :, heads[h]], NT,
                                           preferred_element_type=F32)
                dKa[px] += lax.dot_general(QT[0:96, heads[h]], D[:, heads[h]], NT, preferred_element_type=F32)
                DQ[:, heads[h]] += jnp.dot(KT[px], D[:, heads[h]], preferred_element_type=F32)
            return 0

        lax.fori_loop(0, qx + 1, block, 0)
        for half in range(2):
            p = qx * 2 + half
            for h in range(4):
                start = h * 256 + half * 128
                dq_src[p, h] = (DQ[:, start : start + 128] * SCALE).astype(BF16)

            @pl.when(p != mine)
            def _():
                dq_move(p, mine).start()

        for b in range(8):
            lanes = slice(b * 128, b * 128 + 128)
            part[qx, b % 2, b // 2, 0:96, :] = (dKa[qx, :, lanes] * LN2).astype(BF16)
            part[qx, b % 2, b // 2, 96:192, :] = dVa[qx, :, lanes].astype(BF16)
        part_move(qx).start()

        @pl.when(i >= 1)
        def _():
            reduce_cores(qx + 1)

        @pl.when(i >= 2)
        def _():
            reduce_z(qx + 2)

        return 0

    lax.fori_loop(0, 4, gradients_of, 0)
    reduce_cores(0)

    dq_in[pl.ds(mine * 4, 4)] = dq_src[mine]

    def arrive_dq(j, _):
        p = lax.rem(mine + j, 8)
        dq_move(p, p).wait_recv()
        return 0

    lax.fori_loop(1, 8, arrive_dq, 0)
    reduce_z(1)

    def flip_back(j, _):
        rows = jnp.concatenate([dq_in[slot_of[j * 4 + i]] for i in range(4)], axis=0)
        dq_buf[:, pl.ds(mult(j * 384, 128), 384)] = rows.T
        return 0

    lax.fori_loop(0, 8, flip_back, 0)
    outgoing = [pltpu.make_async_copy(dq_buf, dq_hbm, s_out.at[0])]
    outgoing[0].start()
    reduce_z(0)
    over_x(lambda px: total_move(px, px).wait_recv())
    for g in range(GROUPS):
        kt[g * WIDTH : (g + 1) * WIDTH, :] = fin[g, 0:96, :]
        vt[g * WIDTH : (g + 1) * WIDTH, :] = fin[g, 96:192, :]
    for j in range(3):
        lanes = slice(j * 128, j * 128 + 128)
        dk_buf[:, lanes] = kt[lanes, :].T
        dv_buf[:, lanes] = vt[lanes, :].T
    outgoing.append(pltpu.make_async_copy(dk_buf, dk_hbm, s_out.at[1]))
    outgoing.append(pltpu.make_async_copy(dv_buf, dv_hbm, s_out.at[2]))
    outgoing[1].start()
    outgoing[2].start()

    def sent(p):
        q_move(p, mine).wait_send()
        g_move(p, mine).wait_send()
        dq_move(p, mine).wait_send()

    def sent_all(j, _):
        sent(lax.rem(mine + j, 8))
        return 0

    lax.fori_loop(1, 8, sent_all, 0)

    def sent_x(px):
        k_along_x(px, x).wait_send()
        v_along_x(px, x).wait_send()
        total_move(px, x).wait_send()

    over_x(sent_x)
    over_z(lambda pz: v_along_z(pz, z).wait_send())
    v_to_core(c).wait_send()

    def sent_z(px, _):
        over_z(lambda pz: k_along_z(px, pz, z).wait_send())
        over_z(lambda pz: sum_along_z(px, pz, z).wait_send())
        k_to_core(px, c).wait_send()
        return 0

    lax.fori_loop(0, 4, sent_z, 0)
    for copy in outgoing:
        copy.wait()


def per_device(queries, key_states, value_states, outputs, out_grad, window_start, head_group):
    in_vmem = pl.BlockSpec(memory_space=VM)
    in_smem = pl.BlockSpec(memory_space=pltpu.SMEM)
    anywhere = pl.BlockSpec(memory_space=pl.ANY)
    shape = jax.ShapeDtypeStruct
    me = lax.axis_index("seq")
    position = (window_start[0] + me * 128 + jnp.arange(128, dtype=jnp.int32)).astype(F32)
    half = ROT_DIM // 2
    frequency = 10000.0 ** (-2.0 * jnp.arange(half, dtype=F32) / ROT_DIM)
    angles = position[None, :] * frequency[:, None]
    cosine, sine = jnp.cos(angles), jnp.sin(angles)
    turn = jnp.stack([jnp.concatenate([cosine, cosine], 0), jnp.concatenate([-sine, sine], 0)])
    ids = jnp.arange(HEADS, dtype=jnp.int32)
    same = (head_group[:, None] == head_group[None, :]) & (ids[None, :] < ids[:, None])
    slot_of = head_group * 8 + jnp.sum(same.astype(jnp.int32), axis=1)
    perm = jnp.sum(jnp.where(slot_of[:, None] == ids[None, :], ids[:, None], 0), axis=0)
    dma = pltpu.SemaphoreType.DMA
    wide = VM((128, 3072), BF16)
    tall = VM((HEADS, WIDTH, 128), BF16)
    small = VM((128, 384), BF16)
    small_t = VM((384, 128), BF16)
    return pl.pallas_call(
        kernel,
        out_shape=(shape((128, 3072), BF16), shape((128, 384), BF16), shape((128, 384), BF16)),
        in_specs=[in_smem, in_smem, in_vmem] + [anywhere] * 5,
        out_specs=(anywhere, anywhere, anywhere),
        scratch_shapes=[
            wide, wide, wide, small, small, tall, tall, tall, small_t, small_t, wide, small, small,
            VM((4, 96, 128), BF16), VM((4, 96, 128), BF16),
            VM((4, 2, 4, 96, 128), BF16), VM((4, 2, 4, 96, 128), BF16),
            VM((8, 384, 128), BF16), VM((8, GRAD_ROWS, 128), BF16),
            VM((8, 384, 128), BF16), VM((8, GRAD_ROWS, 128), BF16),
            VM((1024, 1024), F32), VM((1024, 256), F32), VM((10, 1024, 1024), BF16), VM((1024, 1024), BF16),
            VM((128, 1024), BF16), VM((128, 1024), BF16),
            VM((4, 1024, 128), BF16), VM((4, 1024, 128), BF16), VM((4, 96, 1024), BF16),
            VM((4, 96, 1024), F32), VM((4, 96, 1024), F32), VM((96, 1024), F32),
            VM((10, 1, 1024), F32), VM((4, 1, 1024), F32), VM((4, 1, 1024), F32),
            VM((8, 4, 96, 128), BF16), VM((32, 96, 128), BF16),
            VM((4, 2, 4, 192, 128), BF16), VM((4, 4, 192, 128), BF16), VM((4, 4, 192, 128), BF16),
            VM((4, 192, 128), BF16), VM((4, 192, 128), BF16),
        ]
        + [dma((n,)) for n in (5, 3, 8, 8, 8, 8, 4, 4, 4, 4, 16, 16, 4, 4, 4, 4, 1, 1, 8, 8, 4, 4, 16, 16, 4, 4)],
        compiler_params=pltpu.CompilerParams(
            collective_id=0, has_side_effects=True, vmem_limit_bytes=60 << 20
        ),
        cost_estimate=pl.CostEstimate(flops=8_000_000_000, bytes_accessed=4_000_000, transcendentals=8_400_000),
    )(perm, slot_of, turn, queries, key_states, value_states, outputs, out_grad)


def solution(mesh):
    rows = P(("dp", "seq"), None)
    return jax.shard_map(
        per_device,
        mesh=mesh,
        in_specs=(rows, rows, rows, rows, rows, P("dp"), P()),
        out_specs=(rows, rows, rows),
        check_vma=False,
    )
```

```python
import math

import jax
import jax.numpy as jnp
from jax import lax
from jax.experimental import pallas as pl
from jax.experimental.pallas import tpu as pltpu
from jax.sharding import PartitionSpec as P

HEADS = 32
GROUPS = 4
WIDTH = 96
ROT_DIM = 24
F32 = jnp.float32
BF16 = jnp.bfloat16
LN2 = math.log(2.0)
SCALE = WIDTH**-0.5
NT = (((1,), (1,)), ((), ()))
VM = pltpu.VMEM
GRAD_ROWS = 400


def split3(value):
    high = value.astype(BF16)
    rest = value - high.astype(F32)
    middle = rest.astype(BF16)
    low = (rest - middle.astype(F32)).astype(BF16)
    return high.astype(F32), middle.astype(F32), low.astype(F32)


def kernel(perm, slot_of, turn, q_hbm, k_hbm, v_hbm, o_hbm, g_hbm, dq_hbm, dk_hbm, dv_hbm,
           q_in, g_in, o_in, k_in, v_in, qt, gt, ot, kt, vt, dq_buf, dk_buf, dv_buf,
           ksrc, vsrc, kin, qsrc, gsrc, qin, gin,
           S0, S1, bias, Pm, D, QT, DO, Kn, Vn, KT, dKa, dVa, DQ, mrun, mfin, share,
           dq_src, dq_in, part, cin, zin, tot, fin,
           s_in, s_out, s_q, r_q, s_g, r_g, s_kx, r_kx, s_vx, r_vx, s_kz, r_kz, s_kc, r_kc,
           s_vz, r_vz, s_vc, r_vc, s_d, r_d, s_p, r_p, s_z, r_z, s_f, r_f):
    me = lax.axis_index("seq")
    x = me // 8
    z = (me // 2) % 4
    c = me % 2
    mine = x * 2 + c
    near = z + 1 - 2 * (z % 2)
    far = (z + 2) % 4
    cross = (near + 2) % 4
    mesh_id = pl.DeviceIdType.MESH
    mult = pl.multiple_of

    def at(px, pz, pc):
        return {"seq": px * 8 + pz * 2 + pc}

    def owner_at(p):
        return at(p // 2, z, p % 2)

    def remote(src, dst, send, recv, where):
        return pltpu.make_async_remote_copy(
            src_ref=src, dst_ref=dst, send_sem=send, recv_sem=recv,
            device_id=where, device_id_type=mesh_id,
        )

    def loads():
        pairs = ((k_hbm, k_in), (v_hbm, v_in), (q_hbm, q_in), (g_hbm, g_in), (o_hbm, o_in))
        return [pltpu.make_async_copy(a, b, s_in.at[i]) for i, (a, b) in enumerate(pairs)]

    incoming = loads()
    for copy in incoming:
        copy.start()
    barrier = pltpu.get_barrier_semaphore()
    for j in range(1, 8):
        pl.semaphore_signal(barrier, inc=1, device_id=owner_at(lax.rem(mine + j, 8)), device_id_type=mesh_id)
    for pz in (near, far, cross):
        pl.semaphore_signal(barrier, inc=1, device_id=at(x, pz, c), device_id_type=mesh_id)

    cosine = turn[0]
    sine = turn[1]

    def turned(rows):
        first = rows[0:ROT_DIM]
        swapped = jnp.concatenate([first[12:24], first[0:12]], axis=0)
        return jnp.concatenate([first * cosine + swapped * sine, rows[ROT_DIM:]], axis=0)

    def k_along_x(px, land):
        return remote(ksrc.at[px], kin.at[land, c, z], s_kx.at[px], r_kx.at[land], at(px, z, c))

    def v_along_x(px, land):
        return remote(vsrc.at[px], v_rows(land, c, z), s_vx.at[px], r_vx.at[land], at(px, z, c))

    def v_rows(px, pc, pz):
        return Vn.at[px, pl.ds(mult((pc * 4 + pz) * 128, 128), 128)]

    def k_along_z(px, block, pz):
        return remote(kin.at[px, c, block], kin.at[px, c, block], s_kz.at[px * 4 + pz],
                      r_kz.at[px * 4 + block], at(x, pz, c))

    def v_along_z(px, block, pz):
        return remote(v_rows(px, c, block), v_rows(px, c, block), s_vz.at[px * 4 + pz],
                      r_vz.at[px * 4 + block], at(x, pz, c))

    def k_to_core(px, land):
        return remote(kin.at[px, land], kin.at[px, land], s_kc.at[px], r_kc.at[px], at(x, z, 1 - c))

    def v_to_core(px, land):
        rows = Vn.at[px, pl.ds(mult(land * 512, 128), 512)]
        return remote(rows, rows, s_vc.at[px], r_vc.at[px], at(x, z, 1 - c))

    def q_move(p, land):
        return remote(qsrc.at[p], qin.at[land], s_q.at[p], r_q.at[land], owner_at(p))

    def g_move(p, land):
        return remote(gsrc.at[p], gin.at[land], s_g.at[p], r_g.at[land], owner_at(p))

    def dq_move(p, land):
        return remote(dq_src.at[p], dq_in.at[pl.ds(land * 4, 4)], s_d.at[p], r_d.at[land], owner_at(p))

    def part_move(px):
        return remote(part.at[px, 1 - c], cin.at[px], s_p.at[px], r_p.at[px], at(x, z, 1 - c))

    def sum_along_z(px, block, pz, way):
        return remote(part.at[px, c, block], zin.at[px, way], s_z.at[px * 3 + way], r_z.at[px * 3 + way], at(x, pz, c))

    def total_move(px, land):
        return remote(tot.at[px], fin.at[land], s_f.at[px], r_f.at[land], at(px, z, c))

    def over_x(action):
        for j in range(1, 4):
            action(lax.rem(x + j, 4))

    others = (far, cross, near)

    incoming[0].wait()
    for j in range(3):
        lanes = slice(j * 128, j * 128 + 128)
        kt[lanes, :] = k_in[:, lanes].T
    for g in range(GROUPS):
        ksrc[g] = turned(kt[g * WIDTH : (g + 1) * WIDTH, :].astype(F32)).astype(BF16)
    pl.semaphore_wait(barrier, 10)
    over_x(lambda px: k_along_x(px, x).start())
    kin[x, c, z] = ksrc[x]
    incoming[1].wait()
    value_tail = (lax.broadcasted_iota(jnp.int32, (128, 32), 1) < 3).astype(BF16)
    for g in range(GROUPS):
        vsrc[g] = jnp.concatenate([v_in[:, g * WIDTH : (g + 1) * WIDTH], value_tail], axis=1)
    over_x(lambda px: v_along_x(px, x).start())
    Vn[x, pl.ds(mult((c * 4 + z) * 128, 128), 128), :] = vsrc[x]

    incoming[2].wait()

    def flip_q(j, _):
        rows = q_in[:, pl.ds(mult(j * 384, 128), 384)].T
        for i in range(4):
            qt[j * 4 + i] = rows[i * WIDTH : (i + 1) * WIDTH]
        return 0

    lax.fori_loop(0, 8, flip_q, 0)

    def send_q(j, _):
        p = lax.rem(mine + j, 8)
        for i in range(4):
            rows = qt[perm[p * 4 + i]]
            qsrc[p, i * WIDTH : (i + 1) * WIDTH, :] = (turned(rows.astype(F32)) * (SCALE / LN2)).astype(BF16)

        @pl.when(j < 8)
        def _():
            q_move(p, mine).start()

        return 0

    lax.fori_loop(1, 9, send_q, 0)
    qin[mine] = qsrc[mine]

    def spread_k(px, _):
        @pl.when(px != x)
        def _():
            k_along_x(px, px).wait_recv()

        for pz in others:
            k_along_z(px, z, pz).start()
        return 0

    lax.fori_loop(0, 4, spread_k, 0)

    incoming[3].wait()
    incoming[4].wait()

    def flip_g(j, _):
        lanes = pl.ds(mult(j * 384, 128), 384)
        grads = g_in[:, lanes].T
        outs = o_in[:, lanes].T
        for i in range(4):
            gt[j * 4 + i] = grads[i * WIDTH : (i + 1) * WIDTH]
            ot[j * 4 + i] = outs[i * WIDTH : (i + 1) * WIDTH]
        return 0

    lax.fori_loop(0, 8, flip_g, 0)

    def make_g(j, _):
        p = lax.rem(mine + j, 8)
        deltas = []
        for i in range(4):
            head = perm[p * 4 + i]
            grad = gt[head]
            gsrc[p, i * WIDTH : (i + 1) * WIDTH, :] = grad
            deltas.append(jnp.sum(grad.astype(F32) * ot[head].astype(F32), axis=0, keepdims=True))
        high, middle, low = split3(jnp.concatenate(deltas, axis=0))
        gsrc[p, 384:400, :] = jnp.concatenate(
            [high, middle, low, jnp.zeros((4, 128), F32)], axis=0
        ).astype(BF16)
        return 0

    lax.fori_loop(1, 9, make_g, 0)
    gin[mine] = gsrc[mine]


    def spread_v(px):
        for pz in others:
            v_along_z(px, z, pz).start()

    def send_g(j, _):
        g_move(lax.rem(mine + j, 8), mine).start()
        return 0

    def make_bias(i, _):
        rows = pl.ds(mult(i * 128, 128), 128)
        key_id = lax.broadcasted_iota(jnp.int32, (128, 256), 0) + (i % 4 - z) * 256 + (i // 4) * 128
        bias[0, rows, :] = jnp.zeros((128, 256), F32)
        bias[1, rows, :] = jnp.where(key_id <= lax.broadcasted_iota(jnp.int32, (128, 256), 1), 0.0, -1e30)
        return 0

    lax.fori_loop(0, 8, make_bias, 0)

    def clear(i, _):
        dKa[i] = jnp.zeros((96, 1024), F32)
        dVa[i] = jnp.zeros((96, 1024), F32)
        DQ[i] = jnp.zeros((96, 1024), F32)
        return 0

    lax.fori_loop(0, 4, clear, 0)
    QT[:, 96:128, :] = jnp.zeros((4, 32, 1024), BF16)

    def share_k(px):
        for pz in others:
            k_along_z(px, pz, pz).wait_recv()
        k_to_core(px, c).start()

    heads = [slice(h * 256, h * 256 + 256) for h in range(4)]
    zero_rows = jnp.zeros((32, 128), BF16)

    def ready_k(px):
        k_to_core(px, 1 - c).wait_recv()
        for b in range(8):
            lanes = slice(b * 128, b * 128 + 128)
            keys = kin[px, b // 4, b % 4]
            KT[px, :, lanes] = keys
            Kn[px, lanes, :] = jnp.concatenate([keys, zero_rows], 0).T

    def ready_q(qx):
        for half in range(2):
            p = qx * 2 + half

            @pl.when(p != mine)
            def _():
                q_move(p, p).wait_recv()

        for h in range(4):
            for half in range(2):
                start = h * 256 + half * 128
                QT[qx, 0:96, start : start + 128] = qin[qx * 2 + half, h * 96 : h * 96 + 96, :]

    def place(i):
        qx = jnp.minimum(i, 1) + jnp.clip(i - 2, 0, 1) + jnp.clip(i - 5, 0, 1)
        return qx, i - qx * (qx + 1) // 2

    def weigh(i, h, held, top, before, total):
        qx, px = place(i)
        p = jnp.exp2(held[:, heads[h]] - top)
        Pm[i, :, heads[h]] = p.astype(BF16)
        mrun[i, :, heads[h]] = top
        kept = jnp.where(px == 0, 0.0, total * jnp.exp2(before - top))
        return kept + jnp.sum(p.reshape(128, 8, 256), axis=0)

    def settle(i, state):
        qx, px = place(i)
        for h in range(4):
            mfin[qx, :, heads[h]] = state[h]
            share[qx, :, heads[h]] = 1.0 / jnp.sum(state[4 + h], axis=0, keepdims=True)

    def score_pair(t, state):
        @pl.when(t == 0)
        def _():
            share_k(0)
            ready_q(0)
            ready_q(1)
            ready_k(0)
            lax.fori_loop(1, 8, send_g, 0)

        @pl.when(t == 1)
        def _():
            share_k(1)
            share_k(2)
            ready_q(2)
            ready_k(1)
            over_x(lambda px: v_along_x(px, px).wait_recv())
            spread_v(3)

        @pl.when(t == 2)
        def _():
            share_k(3)
            ready_k(2)
            spread_v(2)

        @pl.when(t == 3)
        def _():
            ready_q(3)
            spread_v(1)

        @pl.when(t == 4)
        def _():
            ready_k(3)
            spread_v(0)
            share_v(3)

        top, total, before = list(state[:4]), list(state[4:8]), list(state[8:12])
        for u in range(2):
            i = 2 * t + u
            qx, px = place(i)
            filled, held = (S0, S1) if u == 0 else (S1, S0)
            diagonal = jnp.where(qx == px, 1, 0)
            new_top = [None] * 4
            last = jnp.maximum(i - 1, 0)
            for h in range(4):
                s = jnp.dot(Kn[px], QT[qx, :, heads[h]], preferred_element_type=F32) + bias[diagonal]
                filled[:, heads[h]] = s
                high = jnp.max(jnp.max(s.reshape(128, 8, 256), axis=0), axis=0, keepdims=True)
                new_top[h] = jnp.maximum(jnp.where(px == 0, -1e30, top[h]), high)
                total[h] = weigh(last, h, held, top[h], before[h], total[h])
            settle(last, top + total)
            before, top = top, new_top
        return tuple(top) + tuple(total) + tuple(before)

    def share_v(px):
        for pz in others:
            v_along_z(px, pz, pz).wait_recv()
        v_to_core(px, c).start()

    S1[...] = jnp.zeros((1024, 1024), F32)
    low = tuple(jnp.full((1, 256), -1e30, F32) for _ in range(4))
    none = tuple(jnp.zeros((8, 256), F32) for _ in range(4))
    zeros = tuple(jnp.zeros((1, 256), F32) for _ in range(4))
    state = lax.fori_loop(0, 5, score_pair, zeros + none + zeros)
    total = [weigh(9, h, S1, state[h], state[8 + h], state[4 + h]) for h in range(4)]
    settle(9, list(state[:4]) + total)

    row_id = lax.broadcasted_iota(jnp.int32, (32, 128), 0)

    def reduce_cores(px):
        part_move(px).wait()

        def add(b, _):
            part[px, c, b] = (part[px, c, b].astype(F32) + cin[px, b].astype(F32)).astype(BF16)
            return 0

        lax.fori_loop(0, 4, add, 0)
        sum_along_z(px, cross, near, 1).start()
        sum_along_z(px, near, near, 0).start()

    def reduce_near(px):
        sum_along_z(px, cross, near, 1).wait_recv()
        sum_along_z(px, cross, near, 1).wait_send()
        part[px, c, far] = (part[px, c, far].astype(F32) + zin[px, 1].astype(F32)).astype(BF16)
        sum_along_z(px, far, far, 2).start()

    def reduce_far(px):
        sum_along_z(px, near, near, 0).wait_recv()
        sum_along_z(px, far, far, 2).wait_recv()
        tot[px] = (part[px, c, z].astype(F32) + zin[px, 0].astype(F32) + zin[px, 2].astype(F32)).astype(BF16)

        @pl.when(px != x)
        def _():
            total_move(px, x).start()

        @pl.when(px == x)
        def _():
            fin[x] = tot[px]

    def gradients(n, _):
        group, rank = place(n)
        px = 3 - group
        turn_round = jnp.clip(group - 2, 0, 1)
        qx = turn_round * lax.rem(x + 1 + rank, 4) + (1 - turn_round) * (3 - rank)

        for number, column in ((0, 3), (1, 2), (3, 1), (6, 0)):
            @pl.when(n == number)
            def _():
                for p in (column * 2, column * 2 + 1):
                    @pl.when(p != mine)
                    def _():
                        g_move(p, p).wait_recv()

                if column > 0:
                    share_v(column - 1)
                v_to_core(column, 1 - c).wait_recv()

        block = qx * (qx + 1) // 2 + px
        factor = jnp.exp2(mrun[block] - mfin[qx]) * share[qx]
        for h in range(4):
            for half in range(2):
                start = h * 256 + half * 128
                scale = factor[:, start : start + 128]
                grad = gin[qx * 2 + half, h * 96 : h * 96 + 96, :]
                DO[0:96, start : start + 128] = (grad.astype(F32) * scale).astype(BF16)
                d = gin[qx * 2 + half, 384:400, :].astype(F32)
                d = -(d[h : h + 1] + d[4 + h : 5 + h] + d[8 + h : 9 + h]) * scale
                high, middle, low = split3(d)
                DO[96:128, start : start + 128] = jnp.where(
                    row_id == 0, high, jnp.where(row_id == 1, middle, jnp.where(row_id == 2, low, 0.0))
                ).astype(BF16)
        for h in range(4):
            for r in range(4):
                rows = slice(r * 256, r * 256 + 256)
                dp = jnp.dot(Vn[px, rows, :], DO[:, heads[h]], preferred_element_type=F32)
                D[rows, heads[h]] = (Pm[block, rows, heads[h]].astype(F32) * dp).astype(BF16)
            dVa[px] += lax.dot_general(DO[0:96, heads[h]], Pm[block, :, heads[h]], NT,
                                       preferred_element_type=F32)
            dKa[px] += lax.dot_general(QT[qx, 0:96, heads[h]], D[:, heads[h]], NT, preferred_element_type=F32)
            DQ[qx, :, heads[h]] += jnp.dot(KT[px], D[:, heads[h]], preferred_element_type=F32)

        @pl.when(px == 0)
        def _():
            for half in range(2):
                p = qx * 2 + half
                for h in range(4):
                    start = h * 256 + half * 128
                    dq_src[p, h] = (DQ[qx, :, start : start + 128] * SCALE).astype(BF16)

                @pl.when(p != mine)
                def _():
                    dq_move(p, mine).start()

        @pl.when(rank == group)
        def _():
            for b in range(8):
                lanes = slice(b * 128, b * 128 + 128)
                part[px, b // 4, b % 4, 0:96, :] = (dKa[px, :, lanes] * LN2).astype(BF16)
                part[px, b // 4, b % 4, 96:192, :] = dVa[px, :, lanes].astype(BF16)
            part_move(px).start()

        def after(number, *steps):
            @pl.when(n == number)
            def _():
                for step, column in steps:
                    step(column)

        after(1, (reduce_cores, 3))
        after(3, (reduce_cores, 2), (reduce_near, 3))
        after(5, (reduce_near, 2), (reduce_far, 3))
        after(6, (reduce_cores, 1))
        after(7, (reduce_far, 2))
        after(8, (reduce_near, 1))
        return 0

    lax.fori_loop(0, 10, gradients, 0)
    reduce_cores(0)
    reduce_far(1)
    reduce_near(0)

    dq_in[pl.ds(mine * 4, 4)] = dq_src[mine]

    def arrive_dq(j, _):
        p = lax.rem(mine + j, 8)
        dq_move(p, p).wait_recv()
        return 0

    lax.fori_loop(1, 8, arrive_dq, 0)
    def flip_back(j, _):
        rows = jnp.concatenate([dq_in[slot_of[j * 4 + i]] for i in range(4)], axis=0)
        dq_buf[:, pl.ds(mult(j * 384, 128), 384)] = rows.T
        return 0

    lax.fori_loop(0, 8, flip_back, 0)
    outgoing = [pltpu.make_async_copy(dq_buf, dq_hbm, s_out.at[0])]
    outgoing[0].start()
    reduce_far(0)
    over_x(lambda px: total_move(px, px).wait_recv())
    for g in range(GROUPS):
        kt[g * WIDTH : (g + 1) * WIDTH, :] = fin[g, 0:96, :]
        vt[g * WIDTH : (g + 1) * WIDTH, :] = fin[g, 96:192, :]
    for j in range(3):
        lanes = slice(j * 128, j * 128 + 128)
        dk_buf[:, lanes] = kt[lanes, :].T
        dv_buf[:, lanes] = vt[lanes, :].T
    outgoing.append(pltpu.make_async_copy(dk_buf, dk_hbm, s_out.at[1]))
    outgoing.append(pltpu.make_async_copy(dv_buf, dv_hbm, s_out.at[2]))
    outgoing[1].start()
    outgoing[2].start()

    def sent(p):
        q_move(p, mine).wait_send()
        g_move(p, mine).wait_send()
        dq_move(p, mine).wait_send()

    def sent_all(j, _):
        sent(lax.rem(mine + j, 8))
        return 0

    lax.fori_loop(1, 8, sent_all, 0)

    def sent_x(px):
        k_along_x(px, x).wait_send()
        v_along_x(px, x).wait_send()
        total_move(px, x).wait_send()

    over_x(sent_x)

    def sent_z(px, _):
        for pz in others:
            k_along_z(px, z, pz).wait_send()
            v_along_z(px, z, pz).wait_send()
        sum_along_z(px, near, near, 0).wait_send()
        sum_along_z(px, far, far, 2).wait_send()
        k_to_core(px, c).wait_send()
        v_to_core(px, c).wait_send()
        return 0

    lax.fori_loop(0, 4, sent_z, 0)
    for copy in outgoing:
        copy.wait()


def per_device(queries, key_states, value_states, outputs, out_grad, window_start, head_group):
    in_vmem = pl.BlockSpec(memory_space=VM)
    in_smem = pl.BlockSpec(memory_space=pltpu.SMEM)
    anywhere = pl.BlockSpec(memory_space=pl.ANY)
    shape = jax.ShapeDtypeStruct
    me = lax.axis_index("seq")
    position = (window_start[0] + me * 128 + jnp.arange(128, dtype=jnp.int32)).astype(F32)
    half = ROT_DIM // 2
    frequency = 10000.0 ** (-2.0 * jnp.arange(half, dtype=F32) / ROT_DIM)
    angles = position[None, :] * frequency[:, None]
    cosine, sine = jnp.cos(angles), jnp.sin(angles)
    turn = jnp.stack([jnp.concatenate([cosine, cosine], 0), jnp.concatenate([-sine, sine], 0)])
    ids = jnp.arange(HEADS, dtype=jnp.int32)
    same = (head_group[:, None] == head_group[None, :]) & (ids[None, :] < ids[:, None])
    slot_of = head_group * 8 + jnp.sum(same.astype(jnp.int32), axis=1)
    perm = jnp.sum(jnp.where(slot_of[:, None] == ids[None, :], ids[:, None], 0), axis=0)
    dma = pltpu.SemaphoreType.DMA
    wide = VM((128, 3072), BF16)
    tall = VM((HEADS, WIDTH, 128), BF16)
    small = VM((128, 384), BF16)
    small_t = VM((384, 128), BF16)
    return pl.pallas_call(
        kernel,
        out_shape=(shape((128, 3072), BF16), shape((128, 384), BF16), shape((128, 384), BF16)),
        in_specs=[in_smem, in_smem, in_vmem] + [anywhere] * 5,
        out_specs=(anywhere, anywhere, anywhere),
        scratch_shapes=[
            wide, wide, wide, small, small, tall, tall, tall, small_t, small_t, wide, small, small,
            VM((4, 96, 128), BF16), VM((4, 128, 128), BF16),
            VM((4, 2, 4, 96, 128), BF16),
            VM((8, 384, 128), BF16), VM((8, GRAD_ROWS, 128), BF16),
            VM((8, 384, 128), BF16), VM((8, GRAD_ROWS, 128), BF16),
            VM((1024, 1024), F32), VM((1024, 1024), F32), VM((2, 1024, 256), F32), VM((10, 1024, 1024), BF16), VM((1024, 1024), BF16),
            VM((4, 128, 1024), BF16), VM((128, 1024), BF16),
            VM((4, 1024, 128), BF16), VM((4, 1024, 128), BF16), VM((4, 96, 1024), BF16),
            VM((4, 96, 1024), F32), VM((4, 96, 1024), F32), VM((4, 96, 1024), F32),
            VM((10, 1, 1024), F32), VM((4, 1, 1024), F32), VM((4, 1, 1024), F32),
            VM((8, 4, 96, 128), BF16), VM((32, 96, 128), BF16),
            VM((4, 2, 4, 192, 128), BF16), VM((4, 4, 192, 128), BF16), VM((4, 3, 192, 128), BF16),
            VM((4, 192, 128), BF16), VM((4, 192, 128), BF16),
        ]
        + [dma((n,)) for n in (5, 3, 8, 8, 8, 8, 4, 4, 4, 4, 16, 16, 4, 4, 16, 16, 4, 4, 8, 8, 4, 4, 12, 12, 4, 4)],
        compiler_params=pltpu.CompilerParams(
            collective_id=0, has_side_effects=True, vmem_limit_bytes=60 << 20
        ),
        cost_estimate=pl.CostEstimate(flops=8_000_000_000, bytes_accessed=4_000_000, transcendentals=8_400_000),
    )(perm, slot_of, turn, queries, key_states, value_states, outputs, out_grad)


def solution(mesh):
    rows = P(("dp", "seq"), None)
    return jax.shard_map(
        per_device,
        mesh=mesh,
        in_specs=(rows, rows, rows, rows, rows, P("dp"), P()),
        out_specs=(rows, rows, rows),
        check_vma=False,
    )
```

```python
import math

import jax
import jax.numpy as jnp
from jax import lax
from jax.experimental import pallas as pl
from jax.experimental.pallas import tpu as pltpu
from jax.sharding import PartitionSpec as P

HEADS = 32
GROUPS = 4
WIDTH = 96
ROT_DIM = 24
F32 = jnp.float32
BF16 = jnp.bfloat16
LN2 = math.log(2.0)
SCALE = WIDTH**-0.5
NT = (((1,), (1,)), ((), ()))
VM = pltpu.VMEM
GRAD_ROWS = 400


def split3(value):
    high = value.astype(BF16)
    rest = value - high.astype(F32)
    middle = rest.astype(BF16)
    low = (rest - middle.astype(F32)).astype(BF16)
    return high.astype(F32), middle.astype(F32), low.astype(F32)


def kernel(perm, slot_of, turn, q_hbm, k_hbm, v_hbm, o_hbm, g_hbm, dq_hbm, dk_hbm, dv_hbm,
           q_in, g_in, o_in, k_in, v_in, qt, gt, ot, kt, vt, dk_buf, dv_buf,
           ksrc, vsrc, kin, qsrc, gsrc, qin, gin,
           S0, S1, bias, Pm, D, QT, DO, Kn, Vn, KT, dKa, dVa, DQ, mrun, mfin, share,
           dq_src, dq_in, part, cin, zin, tot, fin,
           s_in, s_out, s_q, r_q, s_g, r_g, s_kx, r_kx, s_vx, r_vx, s_kz, r_kz, s_kc, r_kc,
           s_vz, r_vz, s_vc, r_vc, s_d, r_d, s_p, r_p, s_z, r_z, s_f, r_f):
    me = lax.axis_index("seq")
    x = me // 8
    z = (me // 2) % 4
    c = me % 2
    mine = x * 2 + c
    near = z + 1 - 2 * (z % 2)
    far = (z + 2) % 4
    cross = (near + 2) % 4
    mesh_id = pl.DeviceIdType.MESH
    mult = pl.multiple_of

    def at(px, pz, pc):
        return {"seq": px * 8 + pz * 2 + pc}

    def owner_at(p):
        return at(p // 2, z, p % 2)

    def remote(src, dst, send, recv, where):
        return pltpu.make_async_remote_copy(
            src_ref=src, dst_ref=dst, send_sem=send, recv_sem=recv,
            device_id=where, device_id_type=mesh_id,
        )

    def loads():
        pairs = ((k_hbm, k_in), (v_hbm, v_in), (q_hbm, q_in), (g_hbm, g_in), (o_hbm, o_in))
        return [pltpu.make_async_copy(a, b, s_in.at[i]) for i, (a, b) in enumerate(pairs)]

    incoming = loads()
    for copy in incoming:
        copy.start()
    barrier = pltpu.get_barrier_semaphore()
    for j in range(1, 8):
        pl.semaphore_signal(barrier, inc=1, device_id=owner_at(lax.rem(mine + j, 8)), device_id_type=mesh_id)
    for pz in (near, far, cross):
        pl.semaphore_signal(barrier, inc=1, device_id=at(x, pz, c), device_id_type=mesh_id)

    cosine = turn[0]
    sine = turn[1]

    def turned(rows):
        first = rows[0:ROT_DIM]
        swapped = jnp.concatenate([first[12:24], first[0:12]], axis=0)
        return jnp.concatenate([first * cosine + swapped * sine, rows[ROT_DIM:]], axis=0)

    def k_along_x(px, land):
        return remote(ksrc.at[px], kin.at[land, c, z], s_kx.at[px], r_kx.at[land], at(px, z, c))

    def v_along_x(px, land):
        return remote(vsrc.at[px], v_rows(land, c, z), s_vx.at[px], r_vx.at[land], at(px, z, c))

    def v_rows(px, pc, pz):
        return Vn.at[px, pl.ds(mult((pc * 4 + pz) * 128, 128), 128)]

    def k_along_z(px, block, pz):
        return remote(kin.at[px, c, block], kin.at[px, c, block], s_kz.at[px * 4 + pz],
                      r_kz.at[px * 4 + block], at(x, pz, c))

    def v_along_z(px, block, pz):
        return remote(v_rows(px, c, block), v_rows(px, c, block), s_vz.at[px * 4 + pz],
                      r_vz.at[px * 4 + block], at(x, pz, c))

    def k_to_core(px, land):
        return remote(kin.at[px, land], kin.at[px, land], s_kc.at[px], r_kc.at[px], at(x, z, 1 - c))

    def v_to_core(px, land):
        rows = Vn.at[px, pl.ds(mult(land * 512, 128), 512)]
        return remote(rows, rows, s_vc.at[px], r_vc.at[px], at(x, z, 1 - c))

    def q_move(p, land):
        return remote(qsrc.at[p], qin.at[land], s_q.at[p], r_q.at[land], owner_at(p))

    def g_move(p, land):
        return remote(gsrc.at[p], gin.at[land], s_g.at[p], r_g.at[land], owner_at(p))

    def dq_move(p, land):
        return remote(dq_src.at[p], dq_in.at[pl.ds(land * 4, 4)], s_d.at[p], r_d.at[land], owner_at(p))

    def part_move(px):
        return remote(part.at[px, 1 - c], cin.at[px], s_p.at[px], r_p.at[px], at(x, z, 1 - c))

    def sum_along_z(px, block, pz, way):
        return remote(part.at[px, c, block], zin.at[px, way], s_z.at[px * 3 + way], r_z.at[px * 3 + way], at(x, pz, c))

    def total_move(px, land):
        return remote(tot.at[px], fin.at[land], s_f.at[px], r_f.at[land], at(px, z, c))

    def over_x(action):
        for j in range(1, 4):
            action(lax.rem(x + j, 4))

    others = (far, cross, near)

    incoming[0].wait()
    for j in range(3):
        lanes = slice(j * 128, j * 128 + 128)
        kt[lanes, :] = k_in[:, lanes].T
    for g in range(GROUPS):
        ksrc[g] = turned(kt[g * WIDTH : (g + 1) * WIDTH, :].astype(F32)).astype(BF16)
    pl.semaphore_wait(barrier, 10)
    over_x(lambda px: k_along_x(px, x).start())
    kin[x, c, z] = ksrc[x]
    incoming[1].wait()
    value_tail = (lax.broadcasted_iota(jnp.int32, (128, 32), 1) < 3).astype(BF16)
    for g in range(GROUPS):
        vsrc[g] = jnp.concatenate([v_in[:, g * WIDTH : (g + 1) * WIDTH], value_tail], axis=1)
    over_x(lambda px: v_along_x(px, x).start())
    Vn[x, pl.ds(mult((c * 4 + z) * 128, 128), 128), :] = vsrc[x]

    incoming[2].wait()

    def flip_q(j, _):
        rows = q_in[:, pl.ds(mult(j * 384, 128), 384)].T
        for i in range(4):
            qt[j * 4 + i] = rows[i * WIDTH : (i + 1) * WIDTH]
        return 0

    lax.fori_loop(0, 8, flip_q, 0)

    def send_q(j, _):
        p = lax.rem(mine + j, 8)
        for i in range(4):
            rows = qt[perm[p * 4 + i]]
            qsrc[p, i * WIDTH : (i + 1) * WIDTH, :] = (turned(rows.astype(F32)) * (SCALE / LN2)).astype(BF16)

        @pl.when(j < 8)
        def _():
            q_move(p, mine).start()

        return 0

    lax.fori_loop(1, 9, send_q, 0)
    qin[mine] = qsrc[mine]

    def spread_k(px, _):
        @pl.when(px != x)
        def _():
            k_along_x(px, px).wait_recv()

        for pz in others:
            k_along_z(px, z, pz).start()
        return 0

    lax.fori_loop(0, 4, spread_k, 0)

    incoming[3].wait()
    incoming[4].wait()

    def flip_g(j, _):
        lanes = pl.ds(mult(j * 384, 128), 384)
        grads = g_in[:, lanes].T
        outs = o_in[:, lanes].T
        for i in range(4):
            gt[j * 4 + i] = grads[i * WIDTH : (i + 1) * WIDTH]
            ot[j * 4 + i] = outs[i * WIDTH : (i + 1) * WIDTH]
        return 0

    lax.fori_loop(0, 8, flip_g, 0)

    def make_g(j, _):
        p = lax.rem(mine + j, 8)
        deltas = []
        for i in range(4):
            head = perm[p * 4 + i]
            grad = gt[head]
            gsrc[p, i * WIDTH : (i + 1) * WIDTH, :] = grad
            deltas.append(jnp.sum(grad.astype(F32) * ot[head].astype(F32), axis=0, keepdims=True))
        high, middle, low = split3(jnp.concatenate(deltas, axis=0))
        gsrc[p, 384:400, :] = jnp.concatenate(
            [high, middle, low, jnp.zeros((4, 128), F32)], axis=0
        ).astype(BF16)
        return 0

    lax.fori_loop(1, 9, make_g, 0)
    gin[mine] = gsrc[mine]


    def spread_v(px):
        for pz in others:
            v_along_z(px, z, pz).start()

    def send_g(j, _):
        g_move(lax.rem(mine + j, 8), mine).start()
        return 0

    def make_bias(i, _):
        rows = pl.ds(mult(i * 128, 128), 128)
        key_id = lax.broadcasted_iota(jnp.int32, (128, 256), 0) + (i % 4 - z) * 256 + (i // 4) * 128
        bias[0, rows, :] = jnp.zeros((128, 256), F32)
        bias[1, rows, :] = jnp.where(key_id <= lax.broadcasted_iota(jnp.int32, (128, 256), 1), 0.0, -1e30)
        return 0

    lax.fori_loop(0, 8, make_bias, 0)

    def clear(i, _):
        dKa[i] = jnp.zeros((96, 1024), F32)
        dVa[i] = jnp.zeros((96, 1024), F32)
        DQ[i] = jnp.zeros((96, 1024), F32)
        return 0

    lax.fori_loop(0, 4, clear, 0)
    QT[:, 96:128, :] = jnp.zeros((4, 32, 1024), BF16)

    def share_k(px):
        for pz in others:
            k_along_z(px, pz, pz).wait_recv()
        k_to_core(px, c).start()

    heads = [slice(h * 256, h * 256 + 256) for h in range(4)]
    zero_rows = jnp.zeros((32, 128), BF16)

    def ready_k(px):
        k_to_core(px, 1 - c).wait_recv()
        for b in range(8):
            lanes = slice(b * 128, b * 128 + 128)
            keys = kin[px, b // 4, b % 4]
            KT[px, :, lanes] = keys
            Kn[px, lanes, :] = jnp.concatenate([keys, zero_rows], 0).T

    def ready_q(qx):
        for half in range(2):
            p = qx * 2 + half

            @pl.when(p != mine)
            def _():
                q_move(p, p).wait_recv()

        for h in range(4):
            for half in range(2):
                start = h * 256 + half * 128
                QT[qx, 0:96, start : start + 128] = qin[qx * 2 + half, h * 96 : h * 96 + 96, :]

    def place(i):
        qx = jnp.minimum(i, 1) + jnp.clip(i - 2, 0, 1) + jnp.clip(i - 5, 0, 1)
        return qx, i - qx * (qx + 1) // 2

    def weigh(i, h, held, top, before, total):
        qx, px = place(i)
        p = jnp.exp2(held[:, heads[h]] - top)
        Pm[i, :, heads[h]] = p.astype(BF16)
        mrun[i, :, heads[h]] = top
        kept = jnp.where(px == 0, 0.0, total * jnp.exp2(before - top))
        return kept + jnp.sum(p.reshape(128, 8, 256), axis=0)

    def settle(i, state):
        qx, px = place(i)
        for h in range(4):
            mfin[qx, :, heads[h]] = state[h]
            share[qx, :, heads[h]] = 1.0 / jnp.sum(state[4 + h], axis=0, keepdims=True)

    def score_pair(t, state):
        @pl.when(t == 0)
        def _():
            share_k(0)
            ready_q(0)
            ready_q(1)
            ready_k(0)
            lax.fori_loop(1, 8, send_g, 0)

        @pl.when(t == 1)
        def _():
            share_k(1)
            share_k(2)
            ready_q(2)
            ready_k(1)
            over_x(lambda px: v_along_x(px, px).wait_recv())
            spread_v(3)

        @pl.when(t == 2)
        def _():
            share_k(3)
            ready_k(2)
            spread_v(2)

        @pl.when(t == 3)
        def _():
            ready_q(3)
            spread_v(1)

        @pl.when(t == 4)
        def _():
            ready_k(3)
            spread_v(0)
            share_v(3)

        top, total, before = list(state[:4]), list(state[4:8]), list(state[8:12])
        for u in range(2):
            i = 2 * t + u
            qx, px = place(i)
            filled, held = (S0, S1) if u == 0 else (S1, S0)
            diagonal = jnp.where(qx == px, 1, 0)
            new_top = [None] * 4
            last = jnp.maximum(i - 1, 0)
            for h in range(4):
                s = jnp.dot(Kn[px], QT[qx, :, heads[h]], preferred_element_type=F32) + bias[diagonal]
                filled[:, heads[h]] = s
                high = jnp.max(jnp.max(s.reshape(128, 8, 256), axis=0), axis=0, keepdims=True)
                new_top[h] = jnp.maximum(jnp.where(px == 0, -1e30, top[h]), high)
                total[h] = weigh(last, h, held, top[h], before[h], total[h])
            settle(last, top + total)
            before, top = top, new_top
        return tuple(top) + tuple(total) + tuple(before)

    def share_v(px):
        for pz in others:
            v_along_z(px, pz, pz).wait_recv()
        v_to_core(px, c).start()

    S1[...] = jnp.zeros((1024, 1024), F32)
    low = tuple(jnp.full((1, 256), -1e30, F32) for _ in range(4))
    none = tuple(jnp.zeros((8, 256), F32) for _ in range(4))
    zeros = tuple(jnp.zeros((1, 256), F32) for _ in range(4))
    state = lax.fori_loop(0, 5, score_pair, zeros + none + zeros)
    total = [weigh(9, h, S1, state[h], state[8 + h], state[4 + h]) for h in range(4)]
    settle(9, list(state[:4]) + total)

    row_id = lax.broadcasted_iota(jnp.int32, (32, 128), 0)

    def reduce_cores(px):
        part_move(px).wait()

        def add(b, _):
            part[px, c, b] = (part[px, c, b].astype(F32) + cin[px, b].astype(F32)).astype(BF16)
            return 0

        lax.fori_loop(0, 4, add, 0)

    def send_two_hops(px):
        reduce_cores(px)
        sum_along_z(px, cross, near, 1).start()
        sum_along_z(px, near, near, 0).start()

    def send_one_hop(px):
        reduce_cores(px)
        sum_along_z(px, far, far, 2).start()
        sum_along_z(px, cross, cross, 1).start()
        sum_along_z(px, near, near, 0).start()

    def reduce_near(px):
        sum_along_z(px, cross, near, 1).wait_recv()
        sum_along_z(px, cross, near, 1).wait_send()
        part[px, c, far] = (part[px, c, far].astype(F32) + zin[px, 1].astype(F32)).astype(BF16)
        sum_along_z(px, far, far, 2).start()

    def reduce_far(px, one_hop=False):
        sum_along_z(px, near, near, 0).wait_recv()
        sum_along_z(px, far, far, 2).wait_recv()
        total = part[px, c, z].astype(F32) + zin[px, 0].astype(F32) + zin[px, 2].astype(F32)
        if one_hop:
            sum_along_z(px, cross, cross, 1).wait_recv()
            total = total + zin[px, 1].astype(F32)
        tot[px] = total.astype(BF16)

        @pl.when(px != x)
        def _():
            total_move(px, x).start()

        @pl.when(px == x)
        def _():
            fin[x] = tot[px]

    def gradients(n, _, late=False):
        group, rank = place(n)
        px = 3 - group
        turn_round = jnp.clip(group - 2, 0, 1)
        qx = turn_round * lax.rem(x + 1 + rank, 4) + (1 - turn_round) * (3 - rank)

        for number, column in ((0, 3), (1, 2), (3, 1), (6, 0)):
            @pl.when(n == number)
            def _():
                for p in (column * 2, column * 2 + 1):
                    @pl.when(p != mine)
                    def _():
                        g_move(p, p).wait_recv()

                if column > 0:
                    share_v(column - 1)
                v_to_core(column, 1 - c).wait_recv()

        block = qx * (qx + 1) // 2 + px
        held = D.at[rank] if late else D.at[0]
        factor = jnp.exp2(mrun[block] - mfin[qx]) * share[qx]
        for h in range(4):
            for half in range(2):
                start = h * 256 + half * 128
                scale = factor[:, start : start + 128]
                grad = gin[qx * 2 + half, h * 96 : h * 96 + 96, :]
                DO[0:96, start : start + 128] = (grad.astype(F32) * scale).astype(BF16)
                d = gin[qx * 2 + half, 384:400, :].astype(F32)
                d = -(d[h : h + 1] + d[4 + h : 5 + h] + d[8 + h : 9 + h]) * scale
                high, middle, low = split3(d)
                DO[96:128, start : start + 128] = jnp.where(
                    row_id == 0, high, jnp.where(row_id == 1, middle, jnp.where(row_id == 2, low, 0.0))
                ).astype(BF16)
        for h in range(4):
            for r in range(4):
                rows = slice(r * 256, r * 256 + 256)
                dp = jnp.dot(Vn[px, rows, :], DO[:, heads[h]], preferred_element_type=F32)
                held[rows, heads[h]] = (Pm[block, rows, heads[h]].astype(F32) * dp).astype(BF16)
            dVa[px] += lax.dot_general(DO[0:96, heads[h]], Pm[block, :, heads[h]], NT,
                                       preferred_element_type=F32)
            dKa[px] += lax.dot_general(QT[qx, 0:96, heads[h]], held[:, heads[h]], NT, preferred_element_type=F32)
            if not late:
                DQ[qx, :, heads[h]] += jnp.dot(KT[px], held[:, heads[h]], preferred_element_type=F32)

        @pl.when(rank == group)
        def _():
            for b in range(8):
                lanes = slice(b * 128, b * 128 + 128)
                part[px, b // 4, b % 4, 0:96, :] = (dKa[px, :, lanes] * LN2).astype(BF16)
                part[px, b // 4, b % 4, 96:192, :] = dVa[px, :, lanes].astype(BF16)
            part_move(px).start()

        def after(number, *steps):
            @pl.when(n == number)
            def _():
                for step, column in steps:
                    step(column)

        after(1, (send_two_hops, 3))
        after(3, (send_two_hops, 2), (reduce_near, 3))
        after(5, (reduce_near, 2), (reduce_far, 3))
        after(6, (send_two_hops, 1))
        after(7, (reduce_far, 2))
        after(8, (reduce_near, 1))
        return 0

    lax.fori_loop(0, 6, gradients, 0)
    lax.fori_loop(6, 10, lambda n, _: gradients(n, _, late=True), 0)

    def late_queries(rank, _):
        qx = lax.rem(x + 1 + rank, 4)
        for h in range(4):
            grad = DQ[qx, :, heads[h]] + jnp.dot(KT[0], D[rank, :, heads[h]], preferred_element_type=F32)
            for half in range(2):
                dq_src[qx * 2 + half, h] = (grad[:, half * 128 : half * 128 + 128] * SCALE).astype(BF16)
        for half in range(2):
            p = qx * 2 + half

            @pl.when(p != mine)
            def _():
                dq_move(p, mine).start()

        return 0

    lax.fori_loop(0, 3, late_queries, 0)
    send_one_hop(0)
    late_queries(3, 0)
    reduce_far(1)
    reduce_far(0, one_hop=True)

    dq_in[pl.ds(mine * 4, 4)] = dq_src[mine]

    def arrive_dq(j, _):
        p = lax.rem(mine + j, 8)
        dq_move(p, p).wait_recv()
        return 0

    lax.fori_loop(1, 8, arrive_dq, 0)
    def flip_back(j, _):
        rows = jnp.concatenate([dq_in[slot_of[j * 4 + i]] for i in range(4)], axis=0)
        q_in[:, pl.ds(mult(j * 384, 128), 384)] = rows.T
        return 0

    lax.fori_loop(0, 8, flip_back, 0)
    outgoing = [pltpu.make_async_copy(q_in, dq_hbm, s_out.at[0])]
    outgoing[0].start()
    sum_along_z(0, cross, cross, 1).wait_send()
    over_x(lambda px: total_move(px, px).wait_recv())
    for g in range(GROUPS):
        kt[g * WIDTH : (g + 1) * WIDTH, :] = fin[g, 0:96, :]
        vt[g * WIDTH : (g + 1) * WIDTH, :] = fin[g, 96:192, :]
    for j in range(3):
        lanes = slice(j * 128, j * 128 + 128)
        dk_buf[:, lanes] = kt[lanes, :].T
        dv_buf[:, lanes] = vt[lanes, :].T
    outgoing.append(pltpu.make_async_copy(dk_buf, dk_hbm, s_out.at[1]))
    outgoing.append(pltpu.make_async_copy(dv_buf, dv_hbm, s_out.at[2]))
    outgoing[1].start()
    outgoing[2].start()

    def sent(p):
        q_move(p, mine).wait_send()
        g_move(p, mine).wait_send()
        dq_move(p, mine).wait_send()

    def sent_all(j, _):
        sent(lax.rem(mine + j, 8))
        return 0

    lax.fori_loop(1, 8, sent_all, 0)

    def sent_x(px):
        k_along_x(px, x).wait_send()
        v_along_x(px, x).wait_send()
        total_move(px, x).wait_send()

    over_x(sent_x)

    def sent_z(px, _):
        for pz in others:
            k_along_z(px, z, pz).wait_send()
            v_along_z(px, z, pz).wait_send()
        sum_along_z(px, near, near, 0).wait_send()
        sum_along_z(px, far, far, 2).wait_send()
        k_to_core(px, c).wait_send()
        v_to_core(px, c).wait_send()
        return 0

    lax.fori_loop(0, 4, sent_z, 0)
    for copy in outgoing:
        copy.wait()


def per_device(queries, key_states, value_states, outputs, out_grad, window_start, head_group):
    in_vmem = pl.BlockSpec(memory_space=VM)
    in_smem = pl.BlockSpec(memory_space=pltpu.SMEM)
    anywhere = pl.BlockSpec(memory_space=pl.ANY)
    shape = jax.ShapeDtypeStruct
    me = lax.axis_index("seq")
    position = (window_start[0] + me * 128 + jnp.arange(128, dtype=jnp.int32)).astype(F32)
    half = ROT_DIM // 2
    frequency = 10000.0 ** (-2.0 * jnp.arange(half, dtype=F32) / ROT_DIM)
    angles = position[None, :] * frequency[:, None]
    cosine, sine = jnp.cos(angles), jnp.sin(angles)
    turn = jnp.stack([jnp.concatenate([cosine, cosine], 0), jnp.concatenate([-sine, sine], 0)])
    ids = jnp.arange(HEADS, dtype=jnp.int32)
    same = (head_group[:, None] == head_group[None, :]) & (ids[None, :] < ids[:, None])
    slot_of = head_group * 8 + jnp.sum(same.astype(jnp.int32), axis=1)
    perm = jnp.sum(jnp.where(slot_of[:, None] == ids[None, :], ids[:, None], 0), axis=0)
    dma = pltpu.SemaphoreType.DMA
    wide = VM((128, 3072), BF16)
    tall = VM((HEADS, WIDTH, 128), BF16)
    small = VM((128, 384), BF16)
    small_t = VM((384, 128), BF16)
    return pl.pallas_call(
        kernel,
        out_shape=(shape((128, 3072), BF16), shape((128, 384), BF16), shape((128, 384), BF16)),
        in_specs=[in_smem, in_smem, in_vmem] + [anywhere] * 5,
        out_specs=(anywhere, anywhere, anywhere),
        scratch_shapes=[
            wide, wide, wide, small, small, tall, tall, tall, small_t, small_t, small, small,
            VM((4, 96, 128), BF16), VM((4, 128, 128), BF16),
            VM((4, 2, 4, 96, 128), BF16),
            VM((8, 384, 128), BF16), VM((8, GRAD_ROWS, 128), BF16),
            VM((8, 384, 128), BF16), VM((8, GRAD_ROWS, 128), BF16),
            VM((1024, 1024), F32), VM((1024, 1024), F32), VM((2, 1024, 256), F32), VM((10, 1024, 1024), BF16), VM((4, 1024, 1024), BF16),
            VM((4, 128, 1024), BF16), VM((128, 1024), BF16),
            VM((4, 1024, 128), BF16), VM((4, 1024, 128), BF16), VM((4, 96, 1024), BF16),
            VM((4, 96, 1024), F32), VM((4, 96, 1024), F32), VM((4, 96, 1024), F32),
            VM((10, 1, 1024), F32), VM((4, 1, 1024), F32), VM((4, 1, 1024), F32),
            VM((8, 4, 96, 128), BF16), VM((32, 96, 128), BF16),
            VM((4, 2, 4, 192, 128), BF16), VM((4, 4, 192, 128), BF16), VM((4, 3, 192, 128), BF16),
            VM((4, 192, 128), BF16), VM((4, 192, 128), BF16),
        ]
        + [dma((n,)) for n in (5, 3, 8, 8, 8, 8, 4, 4, 4, 4, 16, 16, 4, 4, 16, 16, 4, 4, 8, 8, 4, 4, 12, 12, 4, 4)],
        compiler_params=pltpu.CompilerParams(
            collective_id=0, has_side_effects=True, vmem_limit_bytes=62 << 20
        ),
        cost_estimate=pl.CostEstimate(flops=8_000_000_000, bytes_accessed=4_000_000, transcendentals=8_400_000),
    )(perm, slot_of, turn, queries, key_states, value_states, outputs, out_grad)


def solution(mesh):
    rows = P(("dp", "seq"), None)
    return jax.shard_map(
        per_device,
        mesh=mesh,
        in_specs=(rows, rows, rows, rows, rows, P("dp"), P()),
        out_specs=(rows, rows, rows),
        check_vma=False,
    )
```

```python
import math

import jax
import jax.numpy as jnp
from jax import lax
from jax.experimental import pallas as pl
from jax.experimental.pallas import tpu as pltpu
from jax.sharding import PartitionSpec as P

HEADS = 32
GROUPS = 4
WIDTH = 96
ROT_DIM = 24
F32 = jnp.float32
BF16 = jnp.bfloat16
LN2 = math.log(2.0)
SCALE = WIDTH**-0.5
NT = (((1,), (1,)), ((), ()))
VM = pltpu.VMEM
GRAD_ROWS = 400


def split3(value):
    high = value.astype(BF16)
    rest = value - high.astype(F32)
    middle = rest.astype(BF16)
    low = (rest - middle.astype(F32)).astype(BF16)
    return high.astype(F32), middle.astype(F32), low.astype(F32)


def kernel(perm, slot_of, turn, q_hbm, k_hbm, v_hbm, o_hbm, g_hbm, dq_hbm, dk_hbm, dv_hbm,
           q_in, g_in, o_in, k_in, v_in, qt, gt, ot, kt, vt, dk_buf, dv_buf,
           ksrc, vsrc, kin, qsrc, gsrc, qin, gin,
           S0, S1, bias, Pm, D, QT, DO, Kn, Vn, KT, dKa, dVa, DQ, mrun, mfin, share,
           dq_src, dq_in, part, cin, zin, tot, fin,
           s_in, s_out, s_q, r_q, s_g, r_g, s_kx, r_kx, s_vx, r_vx, s_kz, r_kz, s_kc, r_kc,
           s_vz, r_vz, s_vc, r_vc, s_d, r_d, s_p, r_p, s_z, r_z, s_f, r_f):
    me = lax.axis_index("seq")
    x = me // 8
    z = (me // 2) % 4
    c = me % 2
    mine = x * 2 + c
    near = z + 1 - 2 * (z % 2)
    far = (z + 2) % 4
    cross = (near + 2) % 4
    mesh_id = pl.DeviceIdType.MESH
    mult = pl.multiple_of

    def at(px, pz, pc):
        return {"seq": px * 8 + pz * 2 + pc}

    def owner_at(p):
        return at(p // 2, z, p % 2)

    def remote(src, dst, send, recv, where):
        return pltpu.make_async_remote_copy(
            src_ref=src, dst_ref=dst, send_sem=send, recv_sem=recv,
            device_id=where, device_id_type=mesh_id,
        )

    def loads():
        pairs = ((k_hbm, k_in), (v_hbm, v_in), (q_hbm, q_in), (g_hbm, g_in), (o_hbm, o_in))
        return [pltpu.make_async_copy(a, b, s_in.at[i]) for i, (a, b) in enumerate(pairs)]

    incoming = loads()
    for copy in incoming:
        copy.start()
    barrier = pltpu.get_barrier_semaphore()
    for j in range(1, 8):
        pl.semaphore_signal(barrier, inc=1, device_id=owner_at(lax.rem(mine + j, 8)), device_id_type=mesh_id)
    for pz in (near, far, cross):
        pl.semaphore_signal(barrier, inc=1, device_id=at(x, pz, c), device_id_type=mesh_id)

    cosine = turn[0]
    sine = turn[1]

    def turned(rows):
        first = rows[0:ROT_DIM]
        swapped = jnp.concatenate([first[12:24], first[0:12]], axis=0)
        return jnp.concatenate([first * cosine + swapped * sine, rows[ROT_DIM:]], axis=0)

    def k_along_x(px, land):
        return remote(ksrc.at[px], kin.at[land, c, z], s_kx.at[px], r_kx.at[land], at(px, z, c))

    def v_along_x(px, land):
        return remote(vsrc.at[px], v_rows(land, c, z), s_vx.at[px], r_vx.at[land], at(px, z, c))

    def v_rows(px, pc, pz):
        return Vn.at[px, pl.ds(mult((pc * 4 + pz) * 128, 128), 128)]

    def k_along_z(px, block, pz):
        return remote(kin.at[px, c, block], kin.at[px, c, block], s_kz.at[px * 4 + pz],
                      r_kz.at[px * 4 + block], at(x, pz, c))

    def v_along_z(px, block, pz):
        return remote(v_rows(px, c, block), v_rows(px, c, block), s_vz.at[px * 4 + pz],
                      r_vz.at[px * 4 + block], at(x, pz, c))

    def k_to_core(px, land):
        return remote(kin.at[px, land], kin.at[px, land], s_kc.at[px], r_kc.at[px], at(x, z, 1 - c))

    def v_to_core(px, land):
        rows = Vn.at[px, pl.ds(mult(land * 512, 128), 512)]
        return remote(rows, rows, s_vc.at[px], r_vc.at[px], at(x, z, 1 - c))

    def q_move(p, land):
        return remote(qsrc.at[p], qin.at[land], s_q.at[p], r_q.at[land], owner_at(p))

    def g_move(p, land):
        return remote(gsrc.at[p], gin.at[land], s_g.at[p], r_g.at[land], owner_at(p))

    def dq_move(p, land):
        return remote(dq_src.at[p], dq_in.at[pl.ds(land * 4, 4)], s_d.at[p], r_d.at[land], owner_at(p))

    def part_move(px):
        return remote(part.at[px, 1 - c], cin.at[px], s_p.at[px], r_p.at[px], at(x, z, 1 - c))

    def sum_along_z(px, block, pz, way):
        return remote(part.at[px, c, block], zin.at[px, way], s_z.at[px * 3 + way], r_z.at[px * 3 + way], at(x, pz, c))

    def total_move(px, land):
        return remote(tot.at[px], fin.at[land], s_f.at[px], r_f.at[land], at(px, z, c))

    def over_x(action):
        for j in range(1, 4):
            action(lax.rem(x + j, 4))

    others = (far, cross, near)

    incoming[0].wait()
    for j in range(3):
        lanes = slice(j * 128, j * 128 + 128)
        kt[lanes, :] = k_in[:, lanes].T
    for g in range(GROUPS):
        ksrc[g] = turned(kt[g * WIDTH : (g + 1) * WIDTH, :].astype(F32)).astype(BF16)
    pl.semaphore_wait(barrier, 10)
    over_x(lambda px: k_along_x(px, x).start())
    kin[x, c, z] = ksrc[x]
    incoming[1].wait()
    value_tail = (lax.broadcasted_iota(jnp.int32, (128, 32), 1) < 3).astype(BF16)
    for g in range(GROUPS):
        vsrc[g] = jnp.concatenate([v_in[:, g * WIDTH : (g + 1) * WIDTH], value_tail], axis=1)
    over_x(lambda px: v_along_x(px, x).start())
    Vn[x, pl.ds(mult((c * 4 + z) * 128, 128), 128), :] = vsrc[x]

    incoming[2].wait()

    def flip_q(j, _):
        rows = q_in[:, pl.ds(mult(j * 384, 128), 384)].T
        for i in range(4):
            qt[j * 4 + i] = rows[i * WIDTH : (i + 1) * WIDTH]
        return 0

    lax.fori_loop(0, 8, flip_q, 0)

    def send_q(j, _):
        p = lax.rem(mine + j, 8)
        for i in range(4):
            rows = qt[perm[p * 4 + i]]
            qsrc[p, i * WIDTH : (i + 1) * WIDTH, :] = (turned(rows.astype(F32)) * (SCALE / LN2)).astype(BF16)

        @pl.when(j < 8)
        def _():
            q_move(p, mine).start()

        return 0

    lax.fori_loop(1, 9, send_q, 0)
    qin[mine] = qsrc[mine]

    def spread_k(px, _):
        @pl.when(px != x)
        def _():
            k_along_x(px, px).wait_recv()

        for pz in others:
            k_along_z(px, z, pz).start()
        return 0

    lax.fori_loop(0, 4, spread_k, 0)

    incoming[3].wait()
    incoming[4].wait()

    def flip_g(j, _):
        lanes = pl.ds(mult(j * 384, 128), 384)
        grads = g_in[:, lanes].T
        outs = o_in[:, lanes].T
        for i in range(4):
            gt[j * 4 + i] = grads[i * WIDTH : (i + 1) * WIDTH]
            ot[j * 4 + i] = outs[i * WIDTH : (i + 1) * WIDTH]
        return 0

    lax.fori_loop(0, 8, flip_g, 0)

    def make_g(j, _):
        p = lax.rem(mine + j, 8)
        deltas = []
        for i in range(4):
            head = perm[p * 4 + i]
            grad = gt[head]
            gsrc[p, i * WIDTH : (i + 1) * WIDTH, :] = grad
            deltas.append(jnp.sum(grad.astype(F32) * ot[head].astype(F32), axis=0, keepdims=True))
        high, middle, low = split3(jnp.concatenate(deltas, axis=0))
        gsrc[p, 384:400, :] = jnp.concatenate(
            [high, middle, low, jnp.zeros((4, 128), F32)], axis=0
        ).astype(BF16)
        return 0

    lax.fori_loop(1, 9, make_g, 0)
    gin[mine] = gsrc[mine]


    def spread_v(px):
        for pz in others:
            v_along_z(px, z, pz).start()

    def send_g(j, _):
        g_move(lax.rem(mine + j, 8), mine).start()
        return 0

    def make_bias(i, _):
        rows = pl.ds(mult(i * 128, 128), 128)
        key_id = lax.broadcasted_iota(jnp.int32, (128, 256), 0) + (i % 4 - z) * 256 + (i // 4) * 128
        bias[0, rows, :] = jnp.zeros((128, 256), F32)
        bias[1, rows, :] = jnp.where(key_id <= lax.broadcasted_iota(jnp.int32, (128, 256), 1), 0.0, -1e30)
        return 0

    lax.fori_loop(0, 8, make_bias, 0)

    def clear(i, _):
        dKa[i] = jnp.zeros((96, 1024), F32)
        dVa[i] = jnp.zeros((96, 1024), F32)
        DQ[i] = jnp.zeros((96, 1024), F32)
        return 0

    lax.fori_loop(0, 4, clear, 0)
    QT[:, 96:128, :] = jnp.zeros((4, 32, 1024), BF16)

    def share_k(px):
        for pz in others:
            k_along_z(px, pz, pz).wait_recv()
        k_to_core(px, c).start()

    heads = [slice(h * 256, h * 256 + 256) for h in range(4)]
    zero_rows = jnp.zeros((32, 128), BF16)

    def ready_k(px):
        k_to_core(px, 1 - c).wait_recv()
        for b in range(8):
            lanes = slice(b * 128, b * 128 + 128)
            keys = kin[px, b // 4, b % 4]
            KT[px, :, lanes] = keys
            Kn[px, lanes, :] = jnp.concatenate([keys, zero_rows], 0).T

    def ready_q(qx):
        for half in range(2):
            p = qx * 2 + half

            @pl.when(p != mine)
            def _():
                q_move(p, p).wait_recv()

        for h in range(4):
            for half in range(2):
                start = h * 256 + half * 128
                QT[qx, 0:96, start : start + 128] = qin[qx * 2 + half, h * 96 : h * 96 + 96, :]

    def place(i):
        qx = jnp.minimum(i, 1) + jnp.clip(i - 2, 0, 1) + jnp.clip(i - 5, 0, 1)
        return qx, i - qx * (qx + 1) // 2

    def weigh(i, h, held, top, before, total):
        qx, px = place(i)
        p = jnp.exp2(held[:, heads[h]] - top)
        Pm[i, :, heads[h]] = p.astype(BF16)
        mrun[i, :, heads[h]] = top
        kept = jnp.where(px == 0, 0.0, total * jnp.exp2(before - top))
        return kept + jnp.sum(p.reshape(128, 8, 256), axis=0)

    def settle(i, state):
        qx, px = place(i)
        for h in range(4):
            mfin[qx, :, heads[h]] = state[h]
            share[qx, :, heads[h]] = 1.0 / jnp.sum(state[4 + h], axis=0, keepdims=True)

    def score_pair(t, state):
        @pl.when(t == 0)
        def _():
            share_k(0)
            ready_q(0)
            ready_q(1)
            ready_k(0)
            lax.fori_loop(1, 8, send_g, 0)

        @pl.when(t == 1)
        def _():
            share_k(1)
            share_k(2)
            ready_q(2)
            ready_k(1)
            over_x(lambda px: v_along_x(px, px).wait_recv())
            spread_v(3)

        @pl.when(t == 2)
        def _():
            share_k(3)
            ready_k(2)
            spread_v(2)

        @pl.when(t == 3)
        def _():
            ready_q(3)
            spread_v(1)

        @pl.when(t == 4)
        def _():
            ready_k(3)
            spread_v(0)
            share_v(3)

        top, total, before = list(state[:4]), list(state[4:8]), list(state[8:12])
        for u in range(2):
            i = 2 * t + u
            qx, px = place(i)
            filled, held = (S0, S1) if u == 0 else (S1, S0)
            diagonal = jnp.where(qx == px, 1, 0)
            new_top = [None] * 4
            last = jnp.maximum(i - 1, 0)
            for h in range(4):
                s = jnp.dot(Kn[px], QT[qx, :, heads[h]], preferred_element_type=F32) + bias[diagonal]
                filled[:, heads[h]] = s
                high = jnp.max(jnp.max(s.reshape(128, 8, 256), axis=0), axis=0, keepdims=True)
                new_top[h] = jnp.maximum(jnp.where(px == 0, -1e30, top[h]), high)
                total[h] = weigh(last, h, held, top[h], before[h], total[h])
            settle(last, top + total)
            before, top = top, new_top
        return tuple(top) + tuple(total) + tuple(before)

    def share_v(px):
        for pz in others:
            v_along_z(px, pz, pz).wait_recv()
        v_to_core(px, c).start()

    S1[...] = jnp.zeros((1024, 1024), F32)
    low = tuple(jnp.full((1, 256), -1e30, F32) for _ in range(4))
    none = tuple(jnp.zeros((8, 256), F32) for _ in range(4))
    zeros = tuple(jnp.zeros((1, 256), F32) for _ in range(4))
    state = lax.fori_loop(0, 5, score_pair, zeros + none + zeros)
    total = [weigh(9, h, S1, state[h], state[8 + h], state[4 + h]) for h in range(4)]
    settle(9, list(state[:4]) + total)

    row_id = lax.broadcasted_iota(jnp.int32, (32, 128), 0)

    def reduce_cores(px):
        part_move(px).wait()

        def add(b, _):
            part[px, c, b] = (part[px, c, b].astype(F32) + cin[px, b].astype(F32)).astype(BF16)
            return 0

        lax.fori_loop(0, 4, add, 0)

    def send_two_hops(px):
        reduce_cores(px)
        sum_along_z(px, cross, near, 1).start()
        sum_along_z(px, near, near, 0).start()

    def send_one_hop(px):
        reduce_cores(px)
        sum_along_z(px, far, far, 2).start()
        sum_along_z(px, cross, cross, 1).start()
        sum_along_z(px, near, near, 0).start()

    def reduce_near(px):
        sum_along_z(px, cross, near, 1).wait_recv()
        sum_along_z(px, cross, near, 1).wait_send()
        part[px, c, far] = (part[px, c, far].astype(F32) + zin[px, 1].astype(F32)).astype(BF16)
        sum_along_z(px, far, far, 2).start()

    def reduce_far(px, one_hop=False):
        sum_along_z(px, near, near, 0).wait_recv()
        sum_along_z(px, far, far, 2).wait_recv()
        total = part[px, c, z].astype(F32) + zin[px, 0].astype(F32) + zin[px, 2].astype(F32)
        if one_hop:
            sum_along_z(px, cross, cross, 1).wait_recv()
            total = total + zin[px, 1].astype(F32)
        tot[px] = total.astype(BF16)

        @pl.when(px != x)
        def _():
            total_move(px, x).start()

        @pl.when(px == x)
        def _():
            fin[x] = tot[px]

    def gradients(n, _, late=False):
        group, rank = place(n)
        px = 3 - group
        turn_round = jnp.clip(group - 2, 0, 1)
        qx = turn_round * lax.rem(x + 1 + rank, 4) + (1 - turn_round) * (3 - rank)

        for number, column in ((0, 3), (1, 2), (3, 1), (6, 0)):
            @pl.when(n == number)
            def _():
                for p in (column * 2, column * 2 + 1):
                    @pl.when(p != mine)
                    def _():
                        g_move(p, p).wait_recv()

                if column > 0:
                    share_v(column - 1)
                v_to_core(column, 1 - c).wait_recv()

        block = qx * (qx + 1) // 2 + px
        held = D.at[rank] if late else D.at[0]
        factor = jnp.exp2(mrun[block] - mfin[qx]) * share[qx]
        for h in range(4):
            for half in range(2):
                start = h * 256 + half * 128
                scale = factor[:, start : start + 128]
                grad = gin[qx * 2 + half, h * 96 : h * 96 + 96, :]
                DO[0:96, start : start + 128] = (grad.astype(F32) * scale).astype(BF16)
                d = gin[qx * 2 + half, 384:400, :].astype(F32)
                d = -(d[h : h + 1] + d[4 + h : 5 + h] + d[8 + h : 9 + h]) * scale
                high, middle, low = split3(d)
                DO[96:128, start : start + 128] = jnp.where(
                    row_id == 0, high, jnp.where(row_id == 1, middle, jnp.where(row_id == 2, low, 0.0))
                ).astype(BF16)
        for h in range(4):
            for r in range(4):
                rows = slice(r * 256, r * 256 + 256)
                dp = jnp.dot(Vn[px, rows, :], DO[:, heads[h]], preferred_element_type=F32)
                held[rows, heads[h]] = (Pm[block, rows, heads[h]].astype(F32) * dp).astype(BF16)
            dVa[px] += lax.dot_general(DO[0:96, heads[h]], Pm[block, :, heads[h]], NT,
                                       preferred_element_type=F32)
            dKa[px] += lax.dot_general(QT[qx, 0:96, heads[h]], held[:, heads[h]], NT, preferred_element_type=F32)
            if not late:
                DQ[qx, :, heads[h]] += jnp.dot(KT[px], held[:, heads[h]], preferred_element_type=F32)

        @pl.when(rank == group)
        def _():
            for b in range(8):
                lanes = slice(b * 128, b * 128 + 128)
                part[px, b // 4, b % 4, 0:96, :] = (dKa[px, :, lanes] * LN2).astype(BF16)
                part[px, b // 4, b % 4, 96:192, :] = dVa[px, :, lanes].astype(BF16)
            part_move(px).start()

        def after(number, *steps):
            @pl.when(n == number)
            def _():
                for step, column in steps:
                    step(column)

        after(1, (send_two_hops, 3))
        after(3, (send_two_hops, 2), (reduce_near, 3))
        after(5, (reduce_near, 2), (reduce_far, 3))
        after(6, (send_one_hop, 1))
        after(7, (reduce_far, 2))
        return 0

    lax.fori_loop(0, 6, gradients, 0)
    lax.fori_loop(6, 10, lambda n, _: gradients(n, _, late=True), 0)

    def late_queries(rank, _):
        qx = lax.rem(x + 1 + rank, 4)
        for h in range(4):
            grad = DQ[qx, :, heads[h]] + jnp.dot(KT[0], D[rank, :, heads[h]], preferred_element_type=F32)
            for half in range(2):
                dq_src[qx * 2 + half, h] = (grad[:, half * 128 : half * 128 + 128] * SCALE).astype(BF16)
        for half in range(2):
            p = qx * 2 + half

            @pl.when(p != mine)
            def _():
                dq_move(p, mine).start()

        return 0

    lax.fori_loop(0, 3, late_queries, 0)
    send_one_hop(0)
    late_queries(3, 0)
    reduce_far(1, one_hop=True)
    reduce_far(0, one_hop=True)

    dq_in[pl.ds(mine * 4, 4)] = dq_src[mine]

    def arrive_dq(j, _):
        p = lax.rem(mine + j, 8)
        dq_move(p, p).wait_recv()
        return 0

    lax.fori_loop(1, 8, arrive_dq, 0)
    def flip_back(j, _):
        rows = jnp.concatenate([dq_in[slot_of[j * 4 + i]] for i in range(4)], axis=0)
        q_in[:, pl.ds(mult(j * 384, 128), 384)] = rows.T
        return 0

    lax.fori_loop(0, 8, flip_back, 0)
    outgoing = [pltpu.make_async_copy(q_in, dq_hbm, s_out.at[0])]
    outgoing[0].start()
    for px in (0, 1):
        sum_along_z(px, cross, cross, 1).wait_send()
    over_x(lambda px: total_move(px, px).wait_recv())
    for g in range(GROUPS):
        kt[g * WIDTH : (g + 1) * WIDTH, :] = fin[g, 0:96, :]
        vt[g * WIDTH : (g + 1) * WIDTH, :] = fin[g, 96:192, :]
    for j in range(3):
        lanes = slice(j * 128, j * 128 + 128)
        dk_buf[:, lanes] = kt[lanes, :].T
        dv_buf[:, lanes] = vt[lanes, :].T
    outgoing.append(pltpu.make_async_copy(dk_buf, dk_hbm, s_out.at[1]))
    outgoing.append(pltpu.make_async_copy(dv_buf, dv_hbm, s_out.at[2]))
    outgoing[1].start()
    outgoing[2].start()

    def sent(p):
        q_move(p, mine).wait_send()
        g_move(p, mine).wait_send()
        dq_move(p, mine).wait_send()

    def sent_all(j, _):
        sent(lax.rem(mine + j, 8))
        return 0

    lax.fori_loop(1, 8, sent_all, 0)

    def sent_x(px):
        k_along_x(px, x).wait_send()
        v_along_x(px, x).wait_send()
        total_move(px, x).wait_send()

    over_x(sent_x)

    def sent_z(px, _):
        for pz in others:
            k_along_z(px, z, pz).wait_send()
            v_along_z(px, z, pz).wait_send()
        sum_along_z(px, near, near, 0).wait_send()
        sum_along_z(px, far, far, 2).wait_send()
        k_to_core(px, c).wait_send()
        v_to_core(px, c).wait_send()
        return 0

    lax.fori_loop(0, 4, sent_z, 0)
    for copy in outgoing:
        copy.wait()


def per_device(queries, key_states, value_states, outputs, out_grad, window_start, head_group):
    in_vmem = pl.BlockSpec(memory_space=VM)
    in_smem = pl.BlockSpec(memory_space=pltpu.SMEM)
    anywhere = pl.BlockSpec(memory_space=pl.ANY)
    shape = jax.ShapeDtypeStruct
    me = lax.axis_index("seq")
    position = (window_start[0] + me * 128 + jnp.arange(128, dtype=jnp.int32)).astype(F32)
    half = ROT_DIM // 2
    frequency = 10000.0 ** (-2.0 * jnp.arange(half, dtype=F32) / ROT_DIM)
    angles = position[None, :] * frequency[:, None]
    cosine, sine = jnp.cos(angles), jnp.sin(angles)
    turn = jnp.stack([jnp.concatenate([cosine, cosine], 0), jnp.concatenate([-sine, sine], 0)])
    ids = jnp.arange(HEADS, dtype=jnp.int32)
    same = (head_group[:, None] == head_group[None, :]) & (ids[None, :] < ids[:, None])
    slot_of = head_group * 8 + jnp.sum(same.astype(jnp.int32), axis=1)
    perm = jnp.sum(jnp.where(slot_of[:, None] == ids[None, :], ids[:, None], 0), axis=0)
    dma = pltpu.SemaphoreType.DMA
    wide = VM((128, 3072), BF16)
    tall = VM((HEADS, WIDTH, 128), BF16)
    small = VM((128, 384), BF16)
    small_t = VM((384, 128), BF16)
    return pl.pallas_call(
        kernel,
        out_shape=(shape((128, 3072), BF16), shape((128, 384), BF16), shape((128, 384), BF16)),
        in_specs=[in_smem, in_smem, in_vmem] + [anywhere] * 5,
        out_specs=(anywhere, anywhere, anywhere),
        scratch_shapes=[
            wide, wide, wide, small, small, tall, tall, tall, small_t, small_t, small, small,
            VM((4, 96, 128), BF16), VM((4, 128, 128), BF16),
            VM((4, 2, 4, 96, 128), BF16),
            VM((8, 384, 128), BF16), VM((8, GRAD_ROWS, 128), BF16),
            VM((8, 384, 128), BF16), VM((8, GRAD_ROWS, 128), BF16),
            VM((1024, 1024), F32), VM((1024, 1024), F32), VM((2, 1024, 256), F32), VM((10, 1024, 1024), BF16), VM((4, 1024, 1024), BF16),
            VM((4, 128, 1024), BF16), VM((128, 1024), BF16),
            VM((4, 1024, 128), BF16), VM((4, 1024, 128), BF16), VM((4, 96, 1024), BF16),
            VM((4, 96, 1024), F32), VM((4, 96, 1024), F32), VM((4, 96, 1024), F32),
            VM((10, 1, 1024), F32), VM((4, 1, 1024), F32), VM((4, 1, 1024), F32),
            VM((8, 4, 96, 128), BF16), VM((32, 96, 128), BF16),
            VM((4, 2, 4, 192, 128), BF16), VM((4, 4, 192, 128), BF16), VM((4, 3, 192, 128), BF16),
            VM((4, 192, 128), BF16), VM((4, 192, 128), BF16),
        ]
        + [dma((n,)) for n in (5, 3, 8, 8, 8, 8, 4, 4, 4, 4, 16, 16, 4, 4, 16, 16, 4, 4, 8, 8, 4, 4, 12, 12, 4, 4)],
        compiler_params=pltpu.CompilerParams(
            collective_id=0, has_side_effects=True, vmem_limit_bytes=62 << 20
        ),
        cost_estimate=pl.CostEstimate(flops=8_000_000_000, bytes_accessed=4_000_000, transcendentals=8_400_000),
    )(perm, slot_of, turn, queries, key_states, value_states, outputs, out_grad)


def solution(mesh):
    rows = P(("dp", "seq"), None)
    return jax.shard_map(
        per_device,
        mesh=mesh,
        in_specs=(rows, rows, rows, rows, rows, P("dp"), P()),
        out_specs=(rows, rows, rows),
        check_vma=False,
    )
```
